256 devices in a mesh: blk: 32 (over y_hi, z, core), head: 8 (over x, y_lo).
Axes of the slice: x: 4, y: 4 (y_hi: 2, y_lo: 2; y = y_hi * 2 + y_lo), z: 8, core: 2. Of those that a mesh axis runs over, the one named last changes fastest.
Arguments:
- queries: bfloat16 [2048, 128, 128], P('blk', 'head'), may hold values from -8 to 8
- new_keys: bfloat16 [2048, 8, 128], P('blk', 'head'), may hold values from -12 to 12
- new_values: bfloat16 [2048, 8, 128], P('blk', 'head'), may hold values from -16 to 16
- segment_ids: int32 [2048], P('blk'), may hold values from 0 to 7, never falling along the last dimension, each value on 1 to 1088 neighbouring positions
- cache_keys: bfloat16 [8192, 8, 128], P('blk', 'head'), may hold values from -8 to 8
- cache_values: bfloat16 [8192, 8, 128], P('blk', 'head'), may hold values from -6 to 6
- cache_lengths: int32 [32], P('blk'), may hold values from 1 to 256, 6144 in all
- o_weight: bfloat16 [16384, 16384], P('head', 'blk'), may hold values from -0.046875 to 0.046875
Outputs:
- attended: bfloat16 [2048, 128, 128], P('blk', 'head')
- projected: bfloat16 [2048, 16384], P('head', 'blk')
The draws below stay inside these ranges and needn't reach their ends.
Inputs may be any that keep to these rules, and one draw needn't show every extreme that they name: `cache_lengths`: the lengths sum to 6144 and the largest is 256. `segment_ids`: never falling along the tokens; each request holds 1 to 1088 tokens, one exactly 1088.
All inputs are finite; a program needn't handle non-finite values. No bound on the sum of `cache_lengths` on one device may be relied on, other than what follows from the above.
Results may differ from the reference program's by a relative error of at most 0.019.
Values may be sent and summed in bfloat16 or wider, within the bound.
A program may use at most 128 MiB of HBM per device.

```python
import math
import jax
import jax.numpy as jnp
import numpy as np
from jax import lax

QH = 128
KVH = 8
HD = 128
D = 16384
Q_DEV = 64
C_DEV = 256
NEW = 2048
CACHE = 8192
N_BLK = 32


def draw_queries(key, part):
    key = jax.random.fold_in(key, 5)
    values = jnp.clip(jax.random.normal(key, (NEW, QH, HD), jnp.float32), -6.0, 6.0)
    return values.astype(jnp.bfloat16)


def draw_cache_keys(key, part):
    key = jax.random.fold_in(key, 9)
    values = jnp.clip(jax.random.normal(key, (CACHE, KVH, HD), jnp.float32), -6.0, 6.0)
    return values.astype(jnp.bfloat16)


def block_levels(key, shape, shards, smallest, top_value):
    factor_of = 1.0
    for axis_at, blocks in shards:
        heights = jax.random.uniform(jax.random.fold_in(jax.random.fold_in(key, 6), axis_at), (blocks,), jnp.float32, smallest / len(shards), top_value / len(shards))
        factor_of = factor_of * jnp.repeat(jnp.exp(heights), shape[axis_at] // blocks).reshape((-1,) + (1,) * (len(shape) - 1 - axis_at))
    return factor_of


def profile(number_of, total, most, lean):
    portions = [(1 << 20) // math.isqrt(rank ** lean) + 1 for rank in range(2, number_of + 1)]
    spare, holding = total - most - (number_of - 1), [1] * (number_of - 1)
    while spare > 0:
        free = [i for i in range(number_of - 1) if holding[i] < most]
        mass, remaining = sum([portions[i] for i in free]), spare
        for i in free:
            addition = min(most - holding[i], max(1, remaining * portions[i] // mass), spare)
            holding[i] = holding[i] + addition
            spare = spare - addition
    return np.array([most] + holding)


def ragged(key, amount, total, limit, slope):
    if amount == 2:
        one = jax.random.randint(key, (), max(1, total - limit), min(limit, total - 1) + 1)
        return jnp.stack([one, total - one])
    lengths = jnp.asarray(profile(amount, total, limit, slope), jnp.int32)
    couples = (amount - 1) // 2
    giver, sink = lengths[1:1 + 2 * couples:2], lengths[2:2 + 2 * couples:2]
    room = jnp.minimum(giver - 1, limit - sink)
    passed = jax.random.randint(jax.random.fold_in(key, 1), (couples,), 0, 1 << 20) % (room + 1)
    lengths = lengths.at[1:1 + 2 * couples:2].set(giver - passed).at[2:2 + 2 * couples:2].set(sink + passed)
    return lengths[jax.random.permutation(jax.random.fold_in(key, 2), amount)]


def scatter_about(own_key, shape, deviation, limit, shards=(), kind=jnp.bfloat16):
    values = deviation * jax.random.normal(own_key, shape, jnp.float32)
    if shards:
        values = values * block_levels(own_key, shape, shards, -0.22, 0.18)
    return jnp.clip(values, -limit, limit).astype(kind)


def setup_inputs(seed: int = 0) -> dict:
    key_list = jax.random.split(jax.random.key(seed), 9)
    return {
        "queries": draw_queries(jax.random.fold_in(key_list[8], 71), 0),
        "new_keys": scatter_about(key_list[1], (NEW, KVH, HD), 2.0, 12.0, ((0, 32), (1, 8))),
        "new_values": scatter_about(key_list[2], (NEW, KVH, HD), 3.0, 16.0, ((0, 32), (1, 8))),
        "segment_ids": jnp.searchsorted(jnp.cumsum(ragged(key_list[3], 8, NEW, NEW // 2 + Q_DEV, 1)), jnp.arange(NEW), side="right").astype(jnp.int32),
        "cache_keys": draw_cache_keys(jax.random.fold_in(key_list[8], 71), 0),
        "cache_values": scatter_about(key_list[5], (CACHE, KVH, HD), 1.0, 6.0, ((0, 32), (1, 8))),
        "cache_lengths": ragged(key_list[6], N_BLK, (3 * N_BLK * C_DEV) // 4, C_DEV, 2).astype(jnp.int32),
        "o_weight": scatter_about(key_list[7], (QH * HD, D), (QH * HD) ** -0.5, 0.046875, ((0, 8), (1, 32))),
    }


def shard_partial(query_block, key_block, value_block, visible):
    scores = jnp.einsum('ngd,cd->ngc', query_block.astype(jnp.float32), key_block.astype(jnp.float32)) * (1.0 / math.sqrt(HD))
    scores = jnp.where(visible[:, None, :], scores, -jnp.inf)
    highest = lax.optimization_barrier(jnp.max(scores, axis=-1))
    weights = jnp.exp(scores - highest[..., None]).astype(jnp.bfloat16)
    denominator = lax.optimization_barrier(jnp.sum(weights.astype(jnp.float32), axis=-1))
    numerator = jnp.einsum('ngc,cd->ngd', weights.astype(jnp.float32), value_block.astype(jnp.float32))
    return (highest, denominator, numerator)

def merge_pair(first, second):
    joint = jnp.maximum(first[0], second[0])
    older = jnp.exp(first[0] - joint)
    newer = jnp.exp(second[0] - joint)
    return (joint, older * first[1] + newer * second[1], older[..., None] * first[2] + newer[..., None] * second[2])

def reference(queries, new_keys, new_values, segment_ids, cache_keys, cache_values, cache_lengths, o_weight):
    group = QH // KVH
    token_rows = jnp.arange(NEW, dtype=jnp.int32)
    visible_new = (segment_ids[None, :] == segment_ids[:, None]) & (token_rows[None, :] <= token_rows[:, None])
    slot_rows = jnp.arange(C_DEV, dtype=jnp.int32)

    def per_head(head_index):
        query_block = lax.dynamic_slice_in_dim(queries, head_index * group, group, 1)
        new_key = lax.dynamic_index_in_dim(new_keys, head_index, 1, keepdims=False)
        new_value = lax.dynamic_index_in_dim(new_values, head_index, 1, keepdims=False)
        state = shard_partial(query_block, new_key, new_value, visible_new)

        def scan_shard(carry, shard):
            start = (shard * C_DEV).astype(jnp.int32)
            key_rows = lax.dynamic_slice_in_dim(cache_keys, start, C_DEV, 0)
            value_rows = lax.dynamic_slice_in_dim(cache_values, start, C_DEV, 0)
            key_block = lax.dynamic_index_in_dim(key_rows, head_index, 1, keepdims=False)
            value_block = lax.dynamic_index_in_dim(value_rows, head_index, 1, keepdims=False)
            visible = (slot_rows < cache_lengths[shard])[None, :]
            return (merge_pair(carry, shard_partial(query_block, key_block, value_block, visible)), None)
        state, unused = lax.scan(scan_shard, state, jnp.arange(N_BLK, dtype=jnp.int32))
        return (state[2] / state[1][..., None]).astype(jnp.bfloat16)
    stacked = lax.map(per_head, jnp.arange(KVH, dtype=jnp.int32))
    attended = jnp.transpose(stacked, (1, 0, 2, 3)).reshape(NEW, QH, HD)
    projected = jnp.dot(attended.reshape(NEW, QH * HD), o_weight, preferred_element_type=jnp.float32).astype(jnp.bfloat16)
    return (attended, projected)
```

```python
import functools
import math

import jax
import jax.numpy as jnp
from jax import lax
from jax.experimental import pallas as pl
from jax.experimental.pallas import tpu as pltpu
from jax.sharding import PartitionSpec as P

MESH = pl.DeviceIdType.MESH
F32 = jnp.float32
BF16 = jnp.bfloat16

QD = 64
CD = 256
HEADS = 16
HD = 128
ROWS = QD * HEADS
NZ = 8
KN0, VN0, META0, PKT = 2 * CD, 2 * CD + QD, 2 * CD + 2 * QD, 2 * CD + 2 * QD + 16
PAIRS = HEADS // 2
LOW = -1e30
SCALE = math.log2(math.e) / math.sqrt(HD)

KP = CD
KQ_MID = 448
AP = 4
AQ_MID = 6

RCHUNK = 128


def kernel(
    q_hbm, kn_hbm, vn_hbm, seg_ref, kc_hbm, vc_hbm, len_ref, w_hbm,
    att_hbm, out_hbm,
    kv, q_buf, segq, m_buf, acc, w_buf, abuf, att_f32, att_bf, psend, rx, keep, ysend, ry, out_buf,
    in_sem, w_sem, out_sem,
    kz_s, kz_r, ky_s, ky_r, kb_s, kb_r,
    az_s, az_r, ay_s, ay_r,
    x_s, x_r, f_s, f_r, wx_s, wx_r,
):
    b = lax.axis_index("blk")
    h = lax.axis_index("head")
    yh, z, c = b // 16, (b // 2) % NZ, b % 2
    x, yl = h // 2, h % 2
    oy, oc = 1 - yh, 1 - c

    def dev(yh_, z_, c_, x_, yl_):
        return {"blk": yh_ * 16 + z_ * 2 + c_, "head": x_ * 2 + yl_}

    right = dev(yh, (z + 1) % NZ, c, x, yl)
    left = dev(yh, (z + NZ - 1) % NZ, c, x, yl)
    across = dev(oy, z, c, x, yl)
    sibling = dev(yh, z, oc, x, yl)
    beside = dev(yh, z, c, x, 1 - yl)
    ring = (right, left)

    def rdma(src, dst, ss, rs, to):
        return pltpu.make_async_remote_copy(
            src_ref=src, dst_ref=dst, send_sem=ss, recv_sem=rs, device_id=to, device_id_type=MESH
        )

    mine = kv.at[c, yh, z]
    loads = [
        pltpu.make_async_copy(kc_hbm, mine.at[pl.ds(0, CD)], in_sem.at[0]),
        pltpu.make_async_copy(vc_hbm, mine.at[pl.ds(CD, CD)], in_sem.at[1]),
        pltpu.make_async_copy(kn_hbm, mine.at[pl.ds(KN0, QD)], in_sem.at[2]),
        pltpu.make_async_copy(vn_hbm, mine.at[pl.ds(VN0, QD)], in_sem.at[3]),
        pltpu.make_async_copy(q_hbm, q_buf, in_sem.at[4]),
    ]
    for cp in loads:
        cp.start()

    barrier = pltpu.get_barrier_semaphore()
    partners = [right, left, across, sibling, beside]
    for dx in (1, 2, 3):
        for cc in (0, 1):
            partners.append(dev(yh, z, cc, (x + dx) % 4, yl))
    for to in partners:
        pl.semaphore_signal(barrier, inc=1, device_id=to, device_id_type=MESH)

    length = len_ref[0]
    seg_row = seg_ref[...].astype(F32)
    for cp in loads[:4]:
        cp.wait()
    shown = lax.broadcasted_iota(jnp.int32, (CD, HD), 0) < length
    keys = kv[c, yh, z, 0:CD, :].astype(F32)
    kv[c, yh, z, 0:CD, :] = jnp.where(shown, keys, keys[0:1, :]).astype(BF16)
    values = kv[c, yh, z, CD : 2 * CD, :].astype(F32)
    kv[c, yh, z, CD : 2 * CD, :] = jnp.where(shown, values, 0.0).astype(BF16)
    top = lax.broadcasted_iota(jnp.int32, (16, HD), 0) < 8
    kv[c, yh, z, META0:PKT, :] = jnp.where(
        top, jnp.broadcast_to(seg_row, (16, HD)), length.astype(F32)
    ).astype(BF16)

    pl.semaphore_wait(barrier, len(partners))

    class Gather:
        def __init__(self, slot, p, qs, qa, qb, zs, zr, ys, yr, sib=None):
            self.slot, self.p, self.q, self.qa, self.qb = slot, p, qs, qa, qb
            self.zs, self.zr, self.ys, self.yr, self.sib = zs, zr, ys, yr, sib
            self.sent = []

        def z_of(self, d, s):
            return (z + NZ - s) % NZ if d == 0 else (z + s) % NZ

        def part(self, kind, d, s):
            if kind < 2:
                if s == 4 and kind != d:
                    return None
                return self.p
            if s == 4:
                return self.qa if d == 0 else self.qb
            return self.q

        def view(self, kind, d, s):
            zo = self.z_of(d, s)
            pc = self.part(kind, d, s)
            return self.slot(oy if kind == 1 else yh, zo, pc)

        def z_send(self, kind, d, s):
            if self.part(kind, d, s) is None:
                return
            zo = self.z_of(d, s - 1)
            ref = self.slot(oy if kind == 1 else yh, zo, self.part(kind, d, s))
            cp = rdma(ref, ref, self.zs.at[d, s - 1, kind], self.zr.at[d, s - 1, kind], ring[d])
            cp.start()
            self.sent.append(cp)

        def z_wait(self, kind, d, s):
            if self.part(kind, d, s) is None:
                return
            ref = self.view(kind, d, s)
            rdma(ref, ref, self.zs.at[d, s - 1, kind], self.zr.at[d, s - 1, kind], ring[d]).wait_recv()

        def code(self, d, s):
            return 0 if s == 0 else (1 + d * 3 + s - 1 if s < 4 else 7 + d)

        def y_piece(self, d, s):
            return self.q if s < 4 else (self.qa if d == 0 else self.qb)

        def y_send(self, d, s):
            k = self.code(d, s)
            ref = self.slot(yh, self.z_of(d, s), self.y_piece(d, s))
            cp = rdma(ref, ref, self.ys.at[k], self.yr.at[k], across)
            cp.start()
            self.sent.append(cp)

        def y_wait(self, d, s):
            k = self.code(d, s)
            ref = self.slot(oy, self.z_of(d, s), self.y_piece(d, s))
            rdma(ref, ref, self.ys.at[k], self.yr.at[k], across).wait_recv()

        def yp_send(self):
            ref = self.slot(yh, z, self.p)
            cp = rdma(ref, ref, self.ys.at[9], self.yr.at[9], across)
            cp.start()
            self.sent.append(cp)

        def yp_wait(self):
            ref = self.slot(oy, z, self.p)
            rdma(ref, ref, self.ys.at[9], self.yr.at[9], across).wait_recv()

        def b_ref(self, kind, d, s, core):
            pc = self.p if kind < 2 else self.y_piece(d, s)
            return kv.at[core, oy if kind % 2 else yh, self.z_of(d, s), pl.ds(pc[0], pc[1])]

        def b_send(self, kind, d, s):
            if self.sib is None:
                return
            if kind < 2 and s > 0 and self.part(kind, d, s) is None:
                return
            k = self.code(d, s)
            ref = self.b_ref(kind, d, s, c)
            cp = rdma(ref, ref, self.sib[0].at[kind, k], self.sib[1].at[kind, k], sibling)
            cp.start()
            self.sent.append(cp)

        def b_wait(self, d, s):
            for kind in range(4):
                if kind < 2 and s > 0 and self.part(kind, d, s) is None:
                    continue
                k = self.code(d, s)
                ref = self.b_ref(kind, d, s, oc)
                rdma(ref, ref, self.sib[0].at[kind, k], self.sib[1].at[kind, k], sibling).wait_recv()

        def open(self):
            self.yp_send()
            for d in (0, 1):
                self.z_send(0, d, 1)
            self.y_send(0, 0)
            for d in (0, 1):
                self.z_send(2, d, 1)
            self.b_send(0, 0, 0)
            self.b_send(2, 0, 0)

        def middle(self):
            self.yp_wait()
            for d in (0, 1):
                self.z_send(1, d, 1)
            self.b_send(1, 0, 0)

        def step(self, s):
            for kind in (0, 2, 1):
                for d in (0, 1):
                    if self.part(kind, d, s) is None:
                        continue
                    self.z_wait(kind, d, s)
                    if s < 4:
                        self.z_send(kind, d, s + 1)
                    if kind == 2:
                        self.y_send(d, s)
                    self.b_send(kind, d, s)

        def late(self, s):
            for d in (0, 1) if s > 0 else (0,):
                self.y_wait(d, s)
                self.b_send(3, d, s)

        def finish(self):
            for cp in self.sent:
                cp.wait_send()

    def kv_slot(y_, z_, pc):
        return kv.at[c, y_, z_, pl.ds(pc[0], pc[1])]

    gk = Gather(
        kv_slot, (0, KP), (KP, PKT - KP), (KP, KQ_MID - KP), (KQ_MID, PKT - KQ_MID),
        kz_s, kz_r, ky_s, ky_r, (kb_s, kb_r),
    )
    gk.open()

    wl, wx = [], []
    for i in (0, 1):
        half = w_hbm.at[:, pl.ds(i * 256, 256)]
        cp = pltpu.make_async_copy(half, w_buf.at[2 * c + i], w_sem.at[i])
        cp.start()
        wl.append(cp)
        cp = rdma(half, w_buf.at[2 * c + i], wx_s.at[i], wx_r.at[i], sibling)
        cp.start()
        wx.append(cp)

    cols = jnp.broadcast_to(seg_row, (HD, HD)).T[0:QD, :]
    segq[...] = jnp.broadcast_to(cols[:, None, :], (QD, HEADS, HD)).reshape(ROWS, HD)
    m_buf[...] = jnp.full((ROWS, HD), LOW, F32)
    acc[...] = jnp.zeros((ROWS, 2 * HD), F32)
    loads[4].wait()

    lane = lax.broadcasted_iota(jnp.int32, (1, CD), 1)
    lane_blk = (lane // 128) * 16 + (lane // 64) % 2

    def attend(zo, first):
        order = [(0, 0), (0, 1), (1, 0), (1, 1)]
        key_blk = lane_blk + zo * 2
        seg0 = [kv[c_, y_, zo, META0:PKT, :][0:1, :].astype(F32) for y_, c_ in order]
        lens = [kv[c_, y_, zo, META0:PKT, :][8:9, :].astype(F32) for y_, c_ in order]
        low = lax.broadcasted_iota(jnp.int32, (1, HD), 1) < QD
        seg_k = jnp.concatenate([jnp.where(low, seg0[0], seg0[1]), jnp.where(low, seg0[2], seg0[3])], axis=1)
        seg_k = jnp.where(key_blk <= b, seg_k, -1.0)
        slot = lax.broadcasted_iota(jnp.int32, (CD, HD), 0).astype(F32)
        counts = [jnp.where(slot < ln, 1.0, 0.0).astype(BF16) for ln in lens]

        def body(r, carry):
            rows = pl.ds(pl.multiple_of(r * RCHUNK, RCHUNK), RCHUNK)
            q = q_buf[rows, :]
            scores = [
                lax.dot_general(
                    q, kv[c_, y_, zo, 0:CD, :], (((1,), (1,)), ((), ())), preferred_element_type=F32
                )
                for y_, c_ in order
            ]
            fresh = jnp.concatenate([kv[c_, y_, zo, KN0 : KN0 + QD, :] for y_, c_ in order], axis=0)
            s_new = lax.dot_general(q, fresh, (((1,), (1,)), ((), ())), preferred_element_type=F32)
            sq = segq[rows, :]
            sees = jnp.concatenate([sq, sq], axis=1) == seg_k
            if first:
                tok = (lax.broadcasted_iota(jnp.int32, (RCHUNK, CD), 0) + r * RCHUNK) // HEADS
                sees = sees & (key_blk * QD + lane % QD <= tok + b * QD)
            s_new = jnp.where(sees, s_new, LOW)
            scores.append(s_new)
            tops = functools.reduce(jnp.maximum, scores)
            tops = jnp.max(tops, axis=1, keepdims=True)
            m_old = m_buf[rows, :]
            m_new = jnp.maximum(m_old, tops)
            m_buf[rows, :] = m_new
            shrink = jnp.exp2((m_old - m_new) * SCALE)
            base = m_new * SCALE
            base2 = jnp.concatenate([base, base], axis=1)
            total = acc[rows, :] * jnp.concatenate([shrink, shrink], axis=1)
            for i, s in enumerate(scores):
                w = jnp.exp2(s * SCALE - base2).astype(BF16)
                if i < 4:
                    y_, c_ = order[i]
                    rhs = jnp.concatenate([kv[c_, y_, zo, CD : 2 * CD, :], counts[i]], axis=1)
                else:
                    fresh_v = jnp.concatenate(
                        [kv[c_, y_, zo, VN0 : VN0 + QD, :] for y_, c_ in order], axis=0
                    )
                    rhs = jnp.concatenate([fresh_v, jnp.ones((CD, HD), BF16)], axis=1)
                total = total + jnp.dot(w, rhs, preferred_element_type=F32)
            acc[rows, :] = total
            return carry

        lax.fori_loop(0, ROWS // RCHUNK, body, 0)

    gk.middle()
    gk.late(0)
    gk.b_wait(0, 0)
    attend(z, True)
    for s in (1, 2, 3, 4):
        gk.step(s)
        if s > 1:
            for d in (0, 1):
                gk.b_wait(d, s - 1)
                attend(gk.z_of(d, s - 1), False)
        gk.late(s)
    for d in (0, 1):
        gk.b_wait(d, 4)
    attend(gk.z_of(0, 4), False)

    def finish_rows(r, carry):
        rows = pl.ds(pl.multiple_of(r * RCHUNK, RCHUNK), RCHUNK)
        o = acc[rows, 0:HD] / acc[rows, HD : 2 * HD]
        att_f32[rows, :] = o
        att_bf[rows, :] = o.astype(BF16)
        return carry

    lax.fori_loop(0, ROWS // RCHUNK, finish_rows, 0)
    for i in range(HEADS):
        abuf[yh, z, i // 2, :, (i % 2) * HD : (i % 2 + 1) * HD] = att_f32[
            pl.ds(i, QD, stride=HEADS), :
        ].astype(BF16)

    ga = Gather(
        lambda y_, z_, pc: abuf.at[y_, z_, pl.ds(pc[0], pc[1])],
        (0, AP), (AP, PAIRS - AP), (AP, AQ_MID - AP), (AQ_MID, PAIRS - AQ_MID),
        az_s, az_r, ay_s, ay_r,
    )
    ga.open()
    att_out = pltpu.make_async_copy(att_bf, att_hbm, out_sem.at[0])
    att_out.start()
    for cp in wl:
        cp.wait()
    for cp in wx:
        cp.wait()

    x_items = []

    def project(items):
        n_rows = len(items) * QD

        def body(n, carry):
            total = jnp.zeros((n_rows, 256), F32)
            for j in range(PAIRS):
                lhs = jnp.concatenate([abuf[y_, z_, j] for y_, z_ in items], axis=0)
                total = total + jnp.dot(
                    lhs, w_buf[n, j * 256 : (j + 1) * 256, :], preferred_element_type=F32
                )
            for i, (y_, z_) in enumerate(items):
                psend[y_, z_, n] = total[i * QD : (i + 1) * QD].astype(BF16)
            return carry

        lax.fori_loop(0, 4, body, 0)
        for y_, z_ in items:
            owner = 2 * y_ + z_ // 4
            for cc in (0, 1):
                to_c = c if cc == 0 else oc
                src = psend.at[y_, z_, pl.ds(2 * to_c, 2)]
                dst = rx.at[x, c, z_ % 4]
                ss = x_s.at[y_, z_, cc]
                rs = x_r.at[x, c, z_ % 4]
                cp = rdma(src, dst, ss, rs, dev(yh, z, to_c, owner, yl))
                if cc == 1:
                    cp.start()
                else:
                    here = pltpu.make_async_copy(src, dst, rs)

                    @pl.when(owner == x)
                    def _():
                        here.start()

                    @pl.when(owner != x)
                    def _():
                        cp.start()

                x_items.append((cp, owner, cc))

    ga.middle()
    ga.late(0)
    project([(yh, z), (oy, z)])
    for s in (1, 2, 3, 4):
        ga.step(s)
        if s > 1:
            zr, zl = ga.z_of(0, s - 1), ga.z_of(1, s - 1)
            project([(yh, zr), (oy, zr), (yh, zl), (oy, zl)])
        ga.late(s)
    zr = ga.z_of(0, 4)
    project([(yh, zr), (oy, zr)])

    def x_wait(cc, zq):
        for xs in range(4):
            ref = rx.at[xs, cc, zq]
            pltpu.make_async_copy(ref, ref, x_r.at[xs, cc, zq]).wait()

    def x_sum(cc, zq, half):
        total = rx[0, cc, zq, half].astype(F32)
        for xs in range(1, 4):
            total = total + rx[xs, cc, zq, half].astype(F32)
        return total

    sends = []
    for e in (0, 1):
        for cc in (0, 1):
            zq = 2 * (1 - yl) + e
            x_wait(cc, zq)
            for half in (0, 1):
                ysend[e, cc, half] = x_sum(cc, zq, half).astype(BF16)
            cp = rdma(ysend.at[e, cc], ry.at[e, cc], f_s.at[e, cc], f_r.at[e, cc], beside)
            cp.start()
            sends.append(cp)
    for e in (0, 1):
        for cc in (0, 1):
            zq = 2 * yl + e
            x_wait(cc, zq)
            for half in (0, 1):
                keep[e, cc, half] = x_sum(cc, zq, half)
    k = 0
    for e in (0, 1):
        for cc in (0, 1):
            sends[k].wait_recv()
            k += 1
            for half in (0, 1):
                out_buf[(e * 2 + cc) * QD : (e * 2 + cc + 1) * QD, half * 256 : (half + 1) * 256] = (
                    keep[e, cc, half] + ry[e, cc, half].astype(F32)
                ).astype(BF16)
    proj_out = pltpu.make_async_copy(out_buf, out_hbm, out_sem.at[1])
    proj_out.start()

    for cp in sends:
        cp.wait_send()
    for cp, owner, cc in x_items:
        if cc == 1:
            cp.wait_send()
        else:

            @pl.when(owner != x)
            def _():
                cp.wait_send()

    gk.finish()
    ga.finish()
    att_out.wait()
    proj_out.wait()


def per_device(queries, new_keys, new_values, segment_ids, cache_keys, cache_values, cache_lengths, o_weight):
    any_ = pl.BlockSpec(memory_space=pl.ANY)
    vmem = pl.BlockSpec(memory_space=pltpu.VMEM)
    smem = pl.BlockSpec(memory_space=pltpu.SMEM)
    dma = pltpu.SemaphoreType.DMA
    seg2 = jnp.concatenate([segment_ids, segment_ids]).reshape(1, 2 * QD)
    att, out = pl.pallas_call(
        kernel,
        out_shape=(
            jax.ShapeDtypeStruct((ROWS, HD), BF16),
            jax.ShapeDtypeStruct((4 * QD, 512), BF16),
        ),
        in_specs=[any_, any_, any_, vmem, any_, any_, smem, any_],
        out_specs=(any_, any_),
        scratch_shapes=[
            pltpu.VMEM((2, 2, NZ, PKT, HD), BF16),
            pltpu.VMEM((ROWS, HD), BF16),
            pltpu.VMEM((ROWS, HD), F32),
            pltpu.VMEM((ROWS, HD), F32),
            pltpu.VMEM((ROWS, 2 * HD), F32),
            pltpu.VMEM((4, HEADS * HD, 256), BF16),
            pltpu.VMEM((2, NZ, PAIRS, QD, 256), BF16),
            pltpu.VMEM((ROWS, HD), F32),
            pltpu.VMEM((ROWS, HD), BF16),
            pltpu.VMEM((2, NZ, 4, QD, 256), BF16),
            pltpu.VMEM((4, 2, 4, 2, QD, 256), BF16),
            pltpu.VMEM((2, 2, 2, QD, 256), F32),
            pltpu.VMEM((2, 2, 2, QD, 256), BF16),
            pltpu.VMEM((2, 2, 2, QD, 256), BF16),
            pltpu.VMEM((4 * QD, 512), BF16),
            dma((5,)), dma((2,)), dma((2,)),
            dma((2, 4, 3)), dma((2, 4, 3)), dma((10,)), dma((10,)), dma((4, 9)), dma((4, 9)),
            dma((2, 4, 3)), dma((2, 4, 3)), dma((10,)), dma((10,)),
            dma((2, NZ, 2)), dma((4, 2, 4)), dma((2, 2)), dma((2, 2)), dma((2,)), dma((2,)),
        ],
        compiler_params=pltpu.CompilerParams(
            collective_id=0, has_side_effects=True, vmem_limit_bytes=56 << 20
        ),
    )(
        queries.reshape(ROWS, HD),
        new_keys.reshape(QD, HD),
        new_values.reshape(QD, HD),
        seg2,
        cache_keys.reshape(CD, HD),
        cache_values.reshape(CD, HD),
        cache_lengths,
        o_weight,
    )
    return att.reshape(QD, HEADS, HD), out


def solution(mesh):
    return jax.shard_map(
        per_device,
        mesh=mesh,
        in_specs=(
            P("blk", "head", None),
            P("blk", "head", None),
            P("blk", "head", None),
            P("blk"),
            P("blk", "head", None),
            P("blk", "head", None),
            P("blk"),
            P("head", "blk"),
        ),
        out_specs=(P("blk", "head", None), P("head", "blk")),
        check_vma=False,
    )
```

```python
import functools
import math

import jax
import jax.numpy as jnp
from jax import lax
from jax.experimental import pallas as pl
from jax.experimental.pallas import tpu as pltpu
from jax.sharding import PartitionSpec as P

MESH = pl.DeviceIdType.MESH
F32 = jnp.float32
BF16 = jnp.bfloat16

QD = 64
CD = 256
HEADS = 16
HD = 128
ROWS = QD * HEADS
NZ = 8
KN0, VN0, META0, PKT = 2 * CD, 2 * CD + QD, 2 * CD + 2 * QD, 2 * CD + 2 * QD + 16
PAIRS = HEADS // 2
LOW = -1e30
SCALE = math.log2(math.e) / math.sqrt(HD)

KP = 448
KQ_MID = 560
AP = 5
AQ_MID = 6

RCHUNK = 256


def kernel(
    q_hbm, kn_hbm, vn_hbm, seg_ref, kc_hbm, vc_hbm, len_ref, w_hbm,
    att_hbm, out_hbm,
    kv, q_buf, segq, m_buf, acc, sc, m_next, vb, w_buf, abuf, att_f32, att_bf, psend, rx, keep, ysend, ry, out_buf,
    in_sem, w_sem, out_sem,
    kz_s, kz_r, ky_s, ky_r, kb_s, kb_r,
    az_s, az_r, ay_s, ay_r,
    x_s, x_r, f_s, f_r, wx_s, wx_r,
):
    b = lax.axis_index("blk")
    h = lax.axis_index("head")
    yh, z, c = b // 16, (b // 2) % NZ, b % 2
    x, yl = h // 2, h % 2
    oy, oc = 1 - yh, 1 - c

    def dev(yh_, z_, c_, x_, yl_):
        return {"blk": yh_ * 16 + z_ * 2 + c_, "head": x_ * 2 + yl_}

    right = dev(yh, (z + 1) % NZ, c, x, yl)
    left = dev(yh, (z + NZ - 1) % NZ, c, x, yl)
    across = dev(oy, z, c, x, yl)
    sibling = dev(yh, z, oc, x, yl)
    beside = dev(yh, z, c, x, 1 - yl)
    ring = (right, left)

    def rdma(src, dst, ss, rs, to):
        return pltpu.make_async_remote_copy(
            src_ref=src, dst_ref=dst, send_sem=ss, recv_sem=rs, device_id=to, device_id_type=MESH
        )

    barrier = pltpu.get_barrier_semaphore()
    partners = [right, left, across, sibling, beside]
    for dx in (1, 2, 3):
        for cc in (0, 1):
            partners.append(dev(yh, z, cc, (x + dx) % 4, yl))
    for to in partners:
        pl.semaphore_signal(barrier, inc=1, device_id=to, device_id_type=MESH)

    mine = kv.at[c, yh, z]
    loads = [
        pltpu.make_async_copy(kc_hbm, mine.at[pl.ds(0, CD)], in_sem.at[0]),
        pltpu.make_async_copy(vc_hbm, mine.at[pl.ds(CD, CD)], in_sem.at[1]),
        pltpu.make_async_copy(kn_hbm, mine.at[pl.ds(KN0, QD)], in_sem.at[2]),
        pltpu.make_async_copy(vn_hbm, mine.at[pl.ds(VN0, QD)], in_sem.at[3]),
        pltpu.make_async_copy(q_hbm, q_buf, in_sem.at[4]),
    ]
    for cp in loads:
        cp.start()

    length = len_ref[0]
    seg_row = seg_ref[...].astype(F32)
    seg_row = jnp.concatenate([seg_row, seg_row], axis=1)
    for cp in loads[:4]:
        cp.wait()
    shown = lax.broadcasted_iota(jnp.int32, (CD, HD), 0) < length
    keys = kv[c, yh, z, 0:CD, :].astype(F32)
    kv[c, yh, z, 0:CD, :] = jnp.where(shown, keys, keys[0:1, :]).astype(BF16)
    values = kv[c, yh, z, CD : 2 * CD, :].astype(F32)
    kv[c, yh, z, CD : 2 * CD, :] = jnp.where(shown, values, 0.0).astype(BF16)
    top = lax.broadcasted_iota(jnp.int32, (16, HD), 0) < 8
    kv[c, yh, z, META0:PKT, :] = jnp.where(
        top, jnp.broadcast_to(seg_row, (16, HD)), length.astype(F32)
    ).astype(BF16)

    pl.semaphore_wait(barrier, len(partners))

    class Gather:
        def __init__(self, slot, p, qs, qa, qb, zs, zr, ys, yr, sib=None):
            self.slot, self.p, self.q, self.qa, self.qb = slot, p, qs, qa, qb
            self.zs, self.zr, self.ys, self.yr, self.sib = zs, zr, ys, yr, sib
            self.sent = []

        def go(self, copy):
            copy().start()
            self.sent.append(copy)

        def z_of(self, d, s):
            return (z + NZ - s) % NZ if d == 0 else (z + s) % NZ

        def part(self, kind, d, s):
            if kind < 2:
                if s == 4 and kind != d:
                    return None
                return self.p
            if s == 4:
                return self.qa if d == 0 else self.qb
            return self.q

        def view(self, kind, d, s):
            return self.slot(oy if kind == 1 else yh, self.z_of(d, s), self.part(kind, d, s))

        def z_send(self, kind, d, s):
            if self.part(kind, d, s) is None:
                return

            def copy():
                ref = self.slot(oy if kind == 1 else yh, self.z_of(d, s - 1), self.part(kind, d, s))
                return rdma(ref, ref, self.zs.at[d, s - 1, kind], self.zr.at[d, s - 1, kind], ring[d])

            self.go(copy)

        def z_wait(self, kind, d, s):
            if self.part(kind, d, s) is None:
                return
            ref = self.view(kind, d, s)
            rdma(ref, ref, self.zs.at[d, s - 1, kind], self.zr.at[d, s - 1, kind], ring[d]).wait_recv()

        def code(self, d, s):
            return 0 if s == 0 else (1 + d * 3 + s - 1 if s < 4 else 7 + d)

        def y_piece(self, d, s):
            return self.q if s < 4 else (self.qa if d == 0 else self.qb)

        def y_send(self, d, s):
            def copy():
                k = self.code(d, s)
                ref = self.slot(yh, self.z_of(d, s), self.y_piece(d, s))
                return rdma(ref, ref, self.ys.at[k], self.yr.at[k], across)

            self.go(copy)

        def y_wait(self, d, s):
            k = self.code(d, s)
            ref = self.slot(oy, self.z_of(d, s), self.y_piece(d, s))
            rdma(ref, ref, self.ys.at[k], self.yr.at[k], across).wait_recv()

        def yp_send(self):
            def copy():
                ref = self.slot(yh, z, self.p)
                return rdma(ref, ref, self.ys.at[9], self.yr.at[9], across)

            self.go(copy)

        def yp_wait(self):
            ref = self.slot(oy, z, self.p)
            rdma(ref, ref, self.ys.at[9], self.yr.at[9], across).wait_recv()

        def b_ref(self, kind, d, s, core):
            pc = self.p if kind < 2 else self.y_piece(d, s)
            return kv.at[core, oy if kind % 2 else yh, self.z_of(d, s), pl.ds(pc[0], pc[1])]

        def b_send(self, kind, d, s):
            if self.sib is None:
                return
            if kind < 2 and s > 0 and self.part(kind, d, s) is None:
                return

            def copy():
                k = self.code(d, s)
                ref = self.b_ref(kind, d, s, c)
                return rdma(ref, ref, self.sib[0].at[kind, k], self.sib[1].at[kind, k], sibling)

            self.go(copy)

        def b_wait(self, d, s):
            for kind in range(4):
                if kind < 2 and s > 0 and self.part(kind, d, s) is None:
                    continue
                k = self.code(d, s)
                ref = self.b_ref(kind, d, s, oc)
                rdma(ref, ref, self.sib[0].at[kind, k], self.sib[1].at[kind, k], sibling).wait_recv()

        def open(self):
            self.yp_send()
            for kind in (2, 0):
                for d in (0, 1):
                    self.z_send(kind, d, 1)
                if kind == 2:
                    self.y_send(0, 0)
                self.b_send(kind, 0, 0)

        def middle(self):
            self.yp_wait()
            for d in (0, 1):
                self.z_send(1, d, 1)
            self.b_send(1, 0, 0)

        def forward(self, kinds, s):
            for kind in kinds:
                for d in (0, 1):
                    if self.part(kind, d, s) is None:
                        continue
                    self.z_wait(kind, d, s)
                    if s < 4:
                        self.z_send(kind, d, s + 1)
                    if kind == 2:
                        self.y_send(d, s)
                    self.b_send(kind, d, s)

        def late(self, s):
            for d in (0, 1) if s > 0 else (0,):
                self.y_wait(d, s)
                self.b_send(3, d, s)

        def finish(self):
            for copy in self.sent:
                copy().wait_send()

    def kv_slot(y_, z_, pc):
        return kv.at[c, y_, z_, pl.ds(pc[0], pc[1])]

    gk = Gather(
        kv_slot, (0, KP), (KP, PKT - KP), (KP, KQ_MID - KP), (KQ_MID, PKT - KQ_MID),
        kz_s, kz_r, ky_s, ky_r, (kb_s, kb_r),
    )
    gk.open()

    cols = jnp.broadcast_to(seg_row, (HD, HD)).T[0:QD, :]
    segq[...] = jnp.broadcast_to(cols[:, None, :], (QD, HEADS, HD)).reshape(ROWS, HD)
    m_buf[...] = jnp.full((ROWS, HD), LOW, F32)
    acc[...] = jnp.zeros((ROWS, 2 * HD), F32)
    loads[4].wait()

    lane = lax.broadcasted_iota(jnp.int32, (1, CD), 1)
    lane_blk = (lane // 128) * 16 + (lane // 64) % 2
    order = [(0, 0), (0, 1), (1, 0), (1, 1)]

    def attend(zo):
        key_blk = lane_blk + zo * 2
        seg0 = [kv[c_, y_, zo, META0:PKT, :][0:1, :].astype(F32) for y_, c_ in order]
        lens = [kv[c_, y_, zo, META0:PKT, :][8:9, :].astype(F32) for y_, c_ in order]
        low = lax.broadcasted_iota(jnp.int32, (1, HD), 1) < QD
        seg_k = jnp.concatenate([jnp.where(low, seg0[0], seg0[1]), jnp.where(low, seg0[2], seg0[3])], axis=1)
        key_row = key_blk * QD + lane % QD
        slot = lax.broadcasted_iota(jnp.int32, (CD, HD), 0).astype(F32)
        for i, (y_, c_) in enumerate(order):
            vb[i * CD : (i + 1) * CD, 0:HD] = kv[c_, y_, zo, CD : 2 * CD, :]
            vb[i * CD : (i + 1) * CD, HD : 2 * HD] = jnp.where(slot < lens[i], 1.0, 0.0).astype(BF16)
            vb[4 * CD + i * QD : 4 * CD + (i + 1) * QD, 0:HD] = kv[c_, y_, zo, VN0 : VN0 + QD, :]
        vb[4 * CD : 5 * CD, HD : 2 * HD] = jnp.ones((CD, HD), BF16)

        def scores(r):
            rows = pl.ds(r * RCHUNK, RCHUNK)
            q = q_buf[rows, :]
            tops = None
            for i in range(5):
                if i < 4:
                    y_, c_ = order[i]
                    keys = kv[c_, y_, zo, 0:CD, :]
                else:
                    keys = jnp.concatenate([kv[c_, y_, zo, KN0 : KN0 + QD, :] for y_, c_ in order], axis=0)
                s = lax.dot_general(q, keys, (((1,), (1,)), ((), ())), preferred_element_type=F32)
                if i == 4:
                    sq = segq[rows, :]
                    sees = jnp.concatenate([sq, sq], axis=1) == seg_k
                    tok = (lax.broadcasted_iota(jnp.int32, (RCHUNK, CD), 0) + r * RCHUNK) // HEADS
                    s = jnp.where(sees & (key_row <= tok + b * QD), s, LOW)
                sc[r % 2, :, i * CD : (i + 1) * CD] = s
                top = jnp.maximum(s[:, 0:HD], s[:, HD : 2 * HD])
                tops = top if tops is None else jnp.maximum(tops, top)
            m_next[r % 2] = jnp.maximum(m_buf[rows, :], jnp.max(tops, axis=1, keepdims=True))

        def weigh(r):
            rows = pl.ds(r * RCHUNK, RCHUNK)
            m_new = m_next[r % 2]
            shrink = jnp.exp2((m_buf[rows, :] - m_new) * SCALE)
            m_buf[rows, :] = m_new
            base = m_new * SCALE
            w = jnp.concatenate(
                [
                    jnp.exp2(sc[r % 2, :, i * HD : (i + 1) * HD] * SCALE - base).astype(BF16)
                    for i in range(10)
                ],
                axis=1,
            )
            acc[rows, :] = acc[rows, :] * jnp.concatenate([shrink, shrink], axis=1) + jnp.dot(
                w, vb[...], preferred_element_type=F32
            )

        n = ROWS // RCHUNK
        scores(0)
        for r in range(n):
            if r + 1 < n:
                scores(r + 1)
            weigh(r)

    def group_z(k):
        s = (k + 1) // 2
        return (z + (1 - 2 * (k % 2)) * s + NZ) % NZ

    def before(g, k, wait):
        if k == 0:
            g.middle()
            g.late(0)
            g.forward((2,), 1)
            if wait:
                g.b_wait(0, 0)
            return
        s = (k + 1) // 2
        if k % 2:
            g.forward((0, 1), s)
            g.late(s)
            if wait:
                g.b_wait(0, s)
                if s == 4:
                    g.b_wait(1, s)
        else:
            g.forward((2,), s + 1)
            if wait:
                g.b_wait(1, s)

    def weights(i):
        half = w_hbm.at[:, pl.ds(i * 256, 256)]
        slot = w_buf.at[2 * c + i]
        here = pltpu.make_async_copy(half, slot, w_sem.at[i])
        return here, rdma(half, slot, wx_s.at[i], wx_r.at[i], sibling)

    def kv_group(k, carry):
        for i in range(8):

            @pl.when(k == i)
            def _():
                before(gk, i, True)
                if i in (2, 3):
                    for cp in weights(i - 2):
                        cp.start()

        attend(group_z(k))
        return carry

    lax.fori_loop(0, 8, kv_group, 0)

    def finish_rows(r, carry):
        rows = pl.ds(pl.multiple_of(r * RCHUNK, RCHUNK), RCHUNK)
        o = acc[rows, 0:HD] / acc[rows, HD : 2 * HD]
        att_f32[rows, :] = o
        att_bf[rows, :] = o.astype(BF16)
        return carry

    lax.fori_loop(0, ROWS // RCHUNK, finish_rows, 0)
    for i in range(HEADS):
        abuf[yh, z, i // 2, :, (i % 2) * HD : (i % 2 + 1) * HD] = att_f32[
            pl.ds(i, QD, stride=HEADS), :
        ].astype(BF16)

    ga = Gather(
        lambda y_, z_, pc: abuf.at[y_, z_, pl.ds(pc[0], pc[1])],
        (0, AP), (AP, PAIRS - AP), (AP, AQ_MID - AP), (AQ_MID, PAIRS - AQ_MID),
        az_s, az_r, ay_s, ay_r,
    )
    ga.open()
    att_out = pltpu.make_async_copy(att_bf, att_hbm, out_sem.at[0])
    att_out.start()
    for i in (0, 1):
        for cp in weights(i):
            cp.wait()

    def x_copy(y_, z_, cc):
        to_c = c if cc == 0 else oc
        owner = 2 * y_ + z_ // 4
        src = psend.at[y_, z_, pl.ds(2 * to_c, 2)]
        dst = rx.at[x, c, z_ % 4]
        rs = x_r.at[x, c, z_ % 4]
        away = rdma(src, dst, x_s.at[y_, z_, cc], rs, dev(yh, z, to_c, owner, yl))
        return away, (src, dst, rs), owner

    def project(zo):
        def body(n, carry):
            total = jnp.zeros((2 * QD, 256), F32)
            for j in range(PAIRS):
                lhs = jnp.concatenate([abuf[yh, zo, j], abuf[oy, zo, j]], axis=0)
                total = total + jnp.dot(
                    lhs, w_buf[n, j * 256 : (j + 1) * 256, :], preferred_element_type=F32
                )
            psend[yh, zo, n] = total[0:QD].astype(BF16)
            psend[oy, zo, n] = total[QD : 2 * QD].astype(BF16)
            return carry

        lax.fori_loop(0, 4, body, 0)
        for y_ in (yh, oy):
            for cc in (0, 1):
                away, here, owner = x_copy(y_, zo, cc)
                if cc == 1:
                    away.start()
                else:

                    @pl.when(owner == x)
                    def _():
                        pltpu.make_async_copy(*here).start()

                    @pl.when(owner != x)
                    def _():
                        away.start()

    u = (z - 4 * (x % 2) + NZ) % NZ
    power = (1 + 3 * (u % 2)) * (1 + 15 * ((u // 2) % 2)) * (1 + 255 * (u // 4))

    def ranked(i):
        table = ((0, 1, 2, 3, 3, 3, 0, 0), (1, 0, 1, 2, 2, 2, 3, 1), (2, 2, 3, 1, 1, 0, 1, 2), (3, 3, 0, 0, 0, 1, 2, 3))[i]
        return (sum(v * 4**n for n, v in enumerate(table)) // power) % 4

    def add_x(i):
        zq = ranked(i)
        e = zq % 2
        for cc in (0, 1):
            for xs in range(4):
                ref = rx.at[xs, cc, zq]
                pltpu.make_async_copy(ref, ref, x_r.at[xs, cc, zq]).wait()
            total = rx[0, cc, zq].astype(F32)
            for xs in range(1, 4):
                total = total + rx[xs, cc, zq].astype(F32)

            @pl.when(zq // 2 == yl)
            def _():
                keep[e, cc] = total

            @pl.when(zq // 2 != yl)
            def _():
                ysend[e, cc] = total.astype(BF16)
                rdma(ysend.at[e, cc], ry.at[e, cc], f_s.at[e, cc], f_r.at[e, cc], beside).start()

    def proj_group(k, carry):
        for i in range(8):

            @pl.when(k == i)
            def _():
                before(ga, i, False)
                if i == 6:
                    add_x(0)

        project(group_z(k))
        return carry

    lax.fori_loop(0, 8, proj_group, 0)
    for i in (1, 2, 3):
        add_x(i)

    sends = [
        rdma(ysend.at[e, cc], ry.at[e, cc], f_s.at[e, cc], f_r.at[e, cc], beside)
        for e in (0, 1)
        for cc in (0, 1)
    ]
    k = 0
    for e in (0, 1):
        for cc in (0, 1):
            sends[k].wait_recv()
            k += 1
            for half in (0, 1):
                out_buf[(e * 2 + cc) * QD : (e * 2 + cc + 1) * QD, half * 256 : (half + 1) * 256] = (
                    keep[e, cc, half] + ry[e, cc, half].astype(F32)
                ).astype(BF16)
    proj_out = pltpu.make_async_copy(out_buf, out_hbm, out_sem.at[1])
    proj_out.start()

    for cp in sends:
        cp.wait_send()

    def x_done(k, carry):
        zo = group_z(k)
        for y_ in (yh, oy):
            for cc in (0, 1):
                away, here, owner = x_copy(y_, zo, cc)
                if cc == 1:
                    away.wait_send()
                else:

                    @pl.when(owner != x)
                    def _():
                        away.wait_send()

        return carry

    lax.fori_loop(0, 8, x_done, 0)
    gk.finish()
    ga.finish()
    att_out.wait()
    proj_out.wait()


def per_device(queries, new_keys, new_values, segment_ids, cache_keys, cache_values, cache_lengths, o_weight):
    any_ = pl.BlockSpec(memory_space=pl.ANY)
    vmem = pl.BlockSpec(memory_space=pltpu.VMEM)
    smem = pl.BlockSpec(memory_space=pltpu.SMEM)
    dma = pltpu.SemaphoreType.DMA
    att, out = pl.pallas_call(
        kernel,
        out_shape=(
            jax.ShapeDtypeStruct((ROWS, HD), BF16),
            jax.ShapeDtypeStruct((4 * QD, 512), BF16),
        ),
        in_specs=[any_, any_, any_, vmem, any_, any_, smem, any_],
        out_specs=(any_, any_),
        scratch_shapes=[
            pltpu.VMEM((2, 2, NZ, PKT, HD), BF16),
            pltpu.VMEM((ROWS, HD), BF16),
            pltpu.VMEM((ROWS, HD), F32),
            pltpu.VMEM((ROWS, HD), F32),
            pltpu.VMEM((ROWS, 2 * HD), F32),
            pltpu.VMEM((2, RCHUNK, 5 * CD), F32),
            pltpu.VMEM((2, RCHUNK, HD), F32),
            pltpu.VMEM((5 * CD, 2 * HD), BF16),
            pltpu.VMEM((4, HEADS * HD, 256), BF16),
            pltpu.VMEM((2, NZ, PAIRS, QD, 256), BF16),
            pltpu.VMEM((ROWS, HD), F32),
            pltpu.VMEM((ROWS, HD), BF16),
            pltpu.VMEM((2, NZ, 4, QD, 256), BF16),
            pltpu.VMEM((4, 2, 4, 2, QD, 256), BF16),
            pltpu.VMEM((2, 2, 2, QD, 256), F32),
            pltpu.VMEM((2, 2, 2, QD, 256), BF16),
            pltpu.VMEM((2, 2, 2, QD, 256), BF16),
            pltpu.VMEM((4 * QD, 512), BF16),
            dma((5,)), dma((2,)), dma((2,)),
            dma((2, 4, 3)), dma((2, 4, 3)), dma((10,)), dma((10,)), dma((4, 9)), dma((4, 9)),
            dma((2, 4, 3)), dma((2, 4, 3)), dma((10,)), dma((10,)),
            dma((2, NZ, 2)), dma((4, 2, 4)), dma((2, 2)), dma((2, 2)), dma((2,)), dma((2,)),
        ],
        compiler_params=pltpu.CompilerParams(
            collective_id=0, has_side_effects=True, vmem_limit_bytes=56 << 20
        ),
    )(
        queries.reshape(ROWS, HD),
        new_keys.reshape(QD, HD),
        new_values.reshape(QD, HD),
        segment_ids.reshape(1, QD),
        cache_keys.reshape(CD, HD),
        cache_values.reshape(CD, HD),
        cache_lengths,
        o_weight,
    )
    return att.reshape(QD, HEADS, HD), out


def solution(mesh):
    return jax.shard_map(
        per_device,
        mesh=mesh,
        in_specs=(
            P("blk", "head", None),
            P("blk", "head", None),
            P("blk", "head", None),
            P("blk"),
            P("blk", "head", None),
            P("blk", "head", None),
            P("blk"),
            P("head", "blk"),
        ),
        out_specs=(P("blk", "head", None), P("head", "blk")),
        check_vma=False,
    )
```

```python
import functools
import math

import jax
import jax.numpy as jnp
from jax import lax
from jax.experimental import pallas as pl
from jax.experimental.pallas import tpu as pltpu
from jax.sharding import PartitionSpec as P

MESH = pl.DeviceIdType.MESH
F32 = jnp.float32
BF16 = jnp.bfloat16

QD = 64
CD = 256
HEADS = 16
HD = 128
ROWS = QD * HEADS
NZ = 8
KN0, VN0, META0, PKT = 2 * CD, 2 * CD + QD, 2 * CD + 2 * QD, 2 * CD + 2 * QD + 16
HALF = QD // 2
PAIRS = HEADS // 2
LOW = -1e30
SCALE = math.log2(math.e) / math.sqrt(HD)

KP = 336
KQ_MID = 496
AP = 4
AQ_MID = 6

RCHUNK = 512


def kernel(
    q_hbm, kn_hbm, vn_hbm, seg_ref, kc_hbm, vc_hbm, len_ref, w_hbm,
    att_hbm, out_hbm,
    kv, q_buf, segq, m_buf, acc, sc, m_next, vb, w_buf, abuf, att_f32, att_bf, psend, relay, rx, keep, ysend, ry, out_buf,
    in_sem, w_sem, out_sem,
    kz_s, kz_r, ky_s, ky_r, kb_s, kb_r,
    az_s, az_r, ay_s, ay_r,
    x_s, x_r, r_r, f_s, f_r, wx_s, wx_r,
):
    b = lax.axis_index("blk")
    h = lax.axis_index("head")
    yh, z, c = b // 16, (b // 2) % NZ, b % 2
    x, yl = h // 2, h % 2
    oy, oc = 1 - yh, 1 - c

    def dev(yh_, z_, c_, x_, yl_):
        return {"blk": yh_ * 16 + z_ * 2 + c_, "head": x_ * 2 + yl_}

    right = dev(yh, (z + 1) % NZ, c, x, yl)
    left = dev(yh, (z + NZ - 1) % NZ, c, x, yl)
    across = dev(oy, z, c, x, yl)
    sibling = dev(yh, z, oc, x, yl)
    beside = dev(yh, z, c, x, 1 - yl)
    ring = (right, left)

    def rdma(src, dst, ss, rs, to):
        return pltpu.make_async_remote_copy(
            src_ref=src, dst_ref=dst, send_sem=ss, recv_sem=rs, device_id=to, device_id_type=MESH
        )

    barrier = pltpu.get_barrier_semaphore()
    partners = [right, left, across, sibling, beside]
    for dx in (1, 3):
        for cc in (0, 1):
            partners.append(dev(yh, z, cc, (x + dx) % 4, yl))
    for to in partners:
        pl.semaphore_signal(barrier, inc=1, device_id=to, device_id_type=MESH)

    mine = kv.at[c, yh, z]
    loads = [
        pltpu.make_async_copy(kc_hbm, mine.at[pl.ds(0, CD)], in_sem.at[0]),
        pltpu.make_async_copy(vc_hbm, mine.at[pl.ds(CD, CD)], in_sem.at[1]),
        pltpu.make_async_copy(kn_hbm, mine.at[pl.ds(KN0, QD)], in_sem.at[2]),
        pltpu.make_async_copy(vn_hbm, mine.at[pl.ds(VN0, QD)], in_sem.at[3]),
        pltpu.make_async_copy(q_hbm, q_buf, in_sem.at[4]),
    ]
    for cp in loads:
        cp.start()

    length = len_ref[0]
    seg_row = seg_ref[...].astype(F32)
    seg_row = jnp.concatenate([seg_row, seg_row], axis=1)
    for cp in loads[:4]:
        cp.wait()
    shown = lax.broadcasted_iota(jnp.int32, (CD, HD), 0) < length
    keys = kv[c, yh, z, 0:CD, :].astype(F32)
    kv[c, yh, z, 0:CD, :] = jnp.where(shown, keys, keys[0:1, :]).astype(BF16)
    values = kv[c, yh, z, CD : 2 * CD, :].astype(F32)
    kv[c, yh, z, CD : 2 * CD, :] = jnp.where(shown, values, 0.0).astype(BF16)
    top = lax.broadcasted_iota(jnp.int32, (16, HD), 0) < 8
    kv[c, yh, z, META0:PKT, :] = jnp.where(
        top, jnp.broadcast_to(seg_row, (16, HD)), length.astype(F32)
    ).astype(BF16)

    pl.semaphore_wait(barrier, len(partners))

    class Gather:
        def __init__(self, slot, p, qs, qa, qb, zs, zr, ys, yr, sib=None, tail=None):
            self.slot, self.p, self.q, self.qa, self.qb = slot, p, qs, qa, qb
            self.zs, self.zr, self.ys, self.yr, self.sib = zs, zr, ys, yr, sib
            self.tail = tail
            self.sent = []

        def go(self, copy):
            copy().start()
            self.sent.append(copy)

        def z_of(self, d, s):
            return (z + NZ - s) % NZ if d == 0 else (z + s) % NZ

        def part(self, kind, d, s):
            if kind == 3:
                return self.tail[1] if self.tail and s == 4 else None
            if kind < 2:
                if s == 4 and kind != d:
                    return None
                return self.tail[0] if self.tail and s == 4 else self.p
            if s == 4:
                return self.qa if d == 0 else self.qb
            return self.q

        def view(self, kind, d, s):
            return self.slot(self.plane(kind, d), self.z_of(d, s), self.part(kind, d, s))

        def plane(self, kind, d):
            return oy if kind == 1 or (kind == 3 and d == 1) else yh

        def z_send(self, kind, d, s):
            if self.part(kind, d, s) is None:
                return

            def copy():
                ref = self.slot(self.plane(kind, d), self.z_of(d, s - 1), self.part(kind, d, s))
                return rdma(ref, ref, self.zs.at[d, s - 1, kind], self.zr.at[d, s - 1, kind], ring[d])

            self.go(copy)

        def z_wait(self, kind, d, s):
            if self.part(kind, d, s) is None:
                return
            ref = self.view(kind, d, s)
            rdma(ref, ref, self.zs.at[d, s - 1, kind], self.zr.at[d, s - 1, kind], ring[d]).wait_recv()

        def code(self, d, s):
            return 0 if s == 0 else (1 + d * 3 + s - 1 if s < 4 else 7 + d)

        def y_piece(self, d, s):
            return self.q if s < 4 else (self.qa if d == 0 else self.qb)

        def y_send(self, d, s):
            def copy():
                k = self.code(d, s)
                ref = self.slot(yh, self.z_of(d, s), self.y_piece(d, s))
                return rdma(ref, ref, self.ys.at[k], self.yr.at[k], across)

            self.go(copy)

        def y_wait(self, d, s):
            k = self.code(d, s)
            ref = self.slot(oy, self.z_of(d, s), self.y_piece(d, s))
            rdma(ref, ref, self.ys.at[k], self.yr.at[k], across).wait_recv()

        def yp_send(self):
            def copy():
                ref = self.slot(yh, z, self.p)
                return rdma(ref, ref, self.ys.at[9], self.yr.at[9], across)

            self.go(copy)

        def yp_wait(self):
            ref = self.slot(oy, z, self.p)
            rdma(ref, ref, self.ys.at[9], self.yr.at[9], across).wait_recv()

        def b_ref(self, kind, d, s, core):
            pc = self.p if kind < 2 else self.y_piece(d, s)
            return kv.at[core, oy if kind % 2 else yh, self.z_of(d, s), pl.ds(pc[0], pc[1])]

        def b_send(self, kind, d, s):
            if self.sib is None:
                return
            if kind < 2 and s > 0 and self.part(kind, d, s) is None:
                return

            def copy():
                k = self.code(d, s)
                ref = self.b_ref(kind, d, s, c)
                return rdma(ref, ref, self.sib[0].at[kind, k], self.sib[1].at[kind, k], sibling)

            self.go(copy)

        def b_wait(self, d, s):
            for kind in range(4):
                if kind < 2 and s > 0 and self.part(kind, d, s) is None:
                    continue
                k = self.code(d, s)
                ref = self.b_ref(kind, d, s, oc)
                rdma(ref, ref, self.sib[0].at[kind, k], self.sib[1].at[kind, k], sibling).wait_recv()

        def open(self):
            self.yp_send()
            for kind in (2, 0):
                for d in (0, 1):
                    self.z_send(kind, d, 1)
                if kind == 2:
                    self.y_send(0, 0)
                self.b_send(kind, 0, 0)

        def middle(self):
            self.yp_wait()
            for d in (0, 1):
                self.z_send(1, d, 1)
            self.b_send(1, 0, 0)

        def forward(self, kinds, s):
            for kind in kinds:
                for d in (0, 1):
                    if self.part(kind, d, s) is None:
                        continue
                    self.z_wait(kind, d, s)
                    if s < 4:
                        self.z_send(kind, d, s + 1)
                    if s == 3 and kind == d:
                        self.z_send(3, d, 4)
                    if kind == 2:
                        self.y_send(d, s)
                    self.b_send(kind, d, s)

        def late(self, s):
            for d in (0, 1) if s > 0 else (0,):
                self.y_wait(d, s)
                self.b_send(3, d, s)

        def finish(self):
            for copy in self.sent:
                copy().wait_send()

    def kv_slot(y_, z_, pc):
        return kv.at[c, y_, z_, pl.ds(pc[0], pc[1])]

    gk = Gather(
        kv_slot, (0, KP), (KP, PKT - KP), (KP, KQ_MID - KP), (KQ_MID, PKT - KQ_MID),
        kz_s, kz_r, ky_s, ky_r, (kb_s, kb_r),
    )
    gk.open()

    cols = jnp.broadcast_to(seg_row, (HD, HD)).T[0:QD, :]
    segq[...] = jnp.broadcast_to(cols[:, None, :], (QD, HEADS, HD)).reshape(ROWS, HD)
    m_buf[...] = jnp.full((ROWS, HD), LOW, F32)
    acc[...] = jnp.zeros((ROWS, 2 * HD), F32)
    loads[4].wait()

    lane = lax.broadcasted_iota(jnp.int32, (1, CD), 1)
    lane_blk = (lane // 128) * 16 + (lane // 64) % 2
    order = [(0, 0), (0, 1), (1, 0), (1, 1)]

    def attend(zo):
        key_blk = lane_blk + zo * 2
        seg0 = [kv[c_, y_, zo, META0:PKT, :][0:1, :].astype(F32) for y_, c_ in order]
        lens = [kv[c_, y_, zo, META0:PKT, :][8:9, :].astype(F32) for y_, c_ in order]
        low = lax.broadcasted_iota(jnp.int32, (1, HD), 1) < QD
        seg_k = jnp.concatenate([jnp.where(low, seg0[0], seg0[1]), jnp.where(low, seg0[2], seg0[3])], axis=1)
        key_row = key_blk * QD + lane % QD
        slot = lax.broadcasted_iota(jnp.int32, (CD, HD), 0).astype(F32)
        for i, (y_, c_) in enumerate(order):
            vb[i * CD : (i + 1) * CD, 0:HD] = kv[c_, y_, zo, CD : 2 * CD, :]
            vb[i * CD : (i + 1) * CD, HD : 2 * HD] = jnp.where(slot < lens[i], 1.0, 0.0).astype(BF16)
            vb[4 * CD + i * QD : 4 * CD + (i + 1) * QD, 0:HD] = kv[c_, y_, zo, VN0 : VN0 + QD, :]
        vb[4 * CD : 5 * CD, HD : 2 * HD] = jnp.ones((CD, HD), BF16)

        def scores(r):
            rows = pl.ds(r * RCHUNK, RCHUNK)
            q = q_buf[rows, :]
            tops = None
            for i in range(5):
                if i < 4:
                    y_, c_ = order[i]
                    keys = kv[c_, y_, zo, 0:CD, :]
                else:
                    keys = jnp.concatenate([kv[c_, y_, zo, KN0 : KN0 + QD, :] for y_, c_ in order], axis=0)
                s = lax.dot_general(q, keys, (((1,), (1,)), ((), ())), preferred_element_type=F32)
                if i == 4:
                    sq = segq[rows, :]
                    sees = jnp.concatenate([sq, sq], axis=1) == seg_k
                    tok = (lax.broadcasted_iota(jnp.int32, (RCHUNK, CD), 0) + r * RCHUNK) // HEADS
                    s = jnp.where(sees & (key_row <= tok + b * QD), s, LOW)
                sc[r % 2, :, i * CD : (i + 1) * CD] = s
                top = jnp.maximum(s[:, 0:HD], s[:, HD : 2 * HD])
                tops = top if tops is None else jnp.maximum(tops, top)
            m_next[r % 2] = jnp.maximum(m_buf[rows, :], jnp.max(tops, axis=1, keepdims=True))

        def weigh(r):
            rows = pl.ds(r * RCHUNK, RCHUNK)
            m_new = m_next[r % 2]
            shrink = jnp.exp2((m_buf[rows, :] - m_new) * SCALE)
            m_buf[rows, :] = m_new
            base = m_new * SCALE
            w = jnp.concatenate(
                [
                    jnp.exp2(sc[r % 2, :, i * HD : (i + 1) * HD] * SCALE - base).astype(BF16)
                    for i in range(10)
                ],
                axis=1,
            )
            acc[rows, :] = acc[rows, :] * jnp.concatenate([shrink, shrink], axis=1) + jnp.dot(
                w, vb[...], preferred_element_type=F32
            )

        n = ROWS // RCHUNK
        scores(0)
        for r in range(n):
            if r + 1 < n:
                scores(r + 1)
            weigh(r)

    def group_z(k):
        s = (k + 1) // 2
        return (z + (1 - 2 * (k % 2)) * s + NZ) % NZ

    def before(g, k, wait):
        q_at = {0: 1, 1: 2, 2: 3, 4: 4}
        if k in q_at:
            g.forward((2,), q_at[k])
        if k == 0:
            g.middle()
            g.late(0)
            if wait:
                g.b_wait(0, 0)
            return
        s = (k + 1) // 2
        if k % 2:
            g.forward((0, 1), s)
        if k in (1, 3, 5, 6):
            g.late((k + 2) // 2)
        if wait:
            g.b_wait(1 - k % 2, s)
            if s == 4:
                g.b_wait(1, s)

    def weights(i):
        half = w_hbm.at[:, pl.ds(i * 256, 256)]
        slot = w_buf.at[2 * c + i]
        here = pltpu.make_async_copy(half, slot, w_sem.at[i])
        return here, rdma(half, slot, wx_s.at[i], wx_r.at[i], sibling)

    def kv_group(k, carry):
        for i in range(8):

            @pl.when(k == i)
            def _():
                before(gk, i, True)
                if i in (2, 3):
                    for cp in weights(i - 2):
                        cp.start()

        attend(group_z(k))
        return carry

    lax.fori_loop(0, 8, kv_group, 0)

    def finish_rows(r, carry):
        rows = pl.ds(pl.multiple_of(r * RCHUNK, RCHUNK), RCHUNK)
        o = acc[rows, 0:HD] / acc[rows, HD : 2 * HD]
        att_f32[rows, :] = o
        att_bf[rows, :] = o.astype(BF16)
        return carry

    lax.fori_loop(0, ROWS // RCHUNK, finish_rows, 0)
    for i in range(HEADS):
        abuf[yh, z, i // 2, :, (i % 2) * HD : (i % 2 + 1) * HD] = att_f32[
            pl.ds(i, QD, stride=HEADS), :
        ].astype(BF16)

    ga = Gather(
        lambda y_, z_, pc: abuf.at[y_, z_, pl.ds(pc[0], pc[1]), pl.ds(pc[2] if len(pc) > 2 else 0, QD // 2 if len(pc) > 2 else QD)],
        (0, AP), (AP, PAIRS - AP), (AP, AQ_MID - AP), (AQ_MID, PAIRS - AQ_MID),
        az_s, az_r, ay_s, ay_r, None, ((0, AP, 0), (0, AP, QD // 2)),
    )
    ga.open()
    att_out = pltpu.make_async_copy(att_bf, att_hbm, out_sem.at[0])
    att_out.start()
    for i in (0, 1):
        for cp in weights(i):
            cp.wait()

    def rows_of(hf):
        return pl.ds(hf * HALF, HALF)

    def to_self(zo, hf):
        return rdma(
            psend.at[x // 2, zo, pl.ds(2 * oc, 2), rows_of(hf)],
            rx.at[2, c, zo % 4, :, rows_of(hf)],
            x_s.at[zo, hf, 0], x_r.at[2, c, zo % 4, hf], sibling,
        )

    def to_relay(zo, hf):
        via = (x + (1 if hf == 0 else 3)) % 4
        return rdma(
            psend.at[1 - x // 2, zo, :, rows_of(hf)],
            relay.at[zo % 4, hf],
            x_s.at[zo, hf, 1], r_r.at[zo % 4, hf], dev(yh, z, c, via, yl),
        )

    def to_owner(zo, hf, up, other):
        owner = (x + (1 if up else 3)) % 4
        to_c = oc if other else c
        relayed = (hf == 0) == up
        return rdma(
            psend.at[owner // 2, zo, pl.ds(2 * to_c, 2), rows_of(hf)],
            rx.at[0 if up else 1, c, zo % 4, :, rows_of(hf)],
            x_s.at[zo, hf, 2 * relayed + other], x_r.at[0 if up else 1, c, zo % 4, hf],
            dev(yh, z, to_c, owner, yl),
        )

    def send_x(zo, halves):
        @pl.when(zo // 4 == x % 2)
        def _():
            for hf in halves:
                to_relay(zo, hf).start()
                to_self(zo, hf).start()

        @pl.when(zo // 4 != x % 2)
        def _():
            for hf in halves:
                for other in (0, 1):
                    to_owner(zo, hf, hf == 1, other).start()

    def relay_x(zo, halves):
        @pl.when(zo // 4 != x % 2)
        def _():
            for hf in halves:
                to_relay(zo, hf).wait_recv()
                y_ = ((x + (1 if hf == 0 else 3)) % 4) // 2
                mine = psend.at[y_, zo]
                rows = slice(hf * HALF, (hf + 1) * HALF)
                mine[:, rows] = (mine[:, rows].astype(F32) + relay[zo % 4, hf].astype(F32)).astype(BF16)
                for other in (0, 1):
                    to_owner(zo, hf, hf == 0, other).start()

    def project(zo, halves):
        first, count = halves[0] * HALF, len(halves) * HALF

        def body(n, carry):
            total = jnp.zeros((2 * count, 256), F32)
            for j in range(PAIRS):
                lhs = jnp.concatenate(
                    [abuf[yh, zo, j, first : first + count], abuf[oy, zo, j, first : first + count]], axis=0
                )
                total = total + jnp.dot(
                    lhs, w_buf[n, j * 256 : (j + 1) * 256, :], preferred_element_type=F32
                )
            psend[yh, zo, n, first : first + count] = total[0:count].astype(BF16)
            psend[oy, zo, n, first : first + count] = total[count : 2 * count].astype(BF16)
            return carry

        lax.fori_loop(0, 4, body, 0)
        send_x(zo, halves)

    u = (z - 4 * (x % 2) + NZ) % NZ
    power = (1 + 3 * (u % 2)) * (1 + 15 * ((u // 2) % 2)) * (1 + 255 * (u // 4))

    def ranked(i):
        table = ((0, 1, 2, 3, 3, 3, 0, 0), (1, 0, 1, 2, 2, 2, 3, 1), (2, 2, 3, 1, 1, 0, 1, 2), (3, 3, 0, 0, 0, 1, 2, 3))[i]
        return (sum(v * 4**n for n, v in enumerate(table)) // power) % 4

    def y_copy(e, cc, hf):
        rows = pl.ds(hf * HALF, HALF)
        return rdma(
            ysend.at[e, cc, :, rows], ry.at[e, cc, :, rows], f_s.at[e, cc, hf], f_r.at[e, cc, hf], beside
        )

    def add_x(i, halves):
        zq = ranked(i)
        e = zq % 2
        first, count = halves[0] * HALF, len(halves) * HALF
        rows = slice(first, first + count)
        for cc in (c, oc):
            for side in (0, 1) if cc is c else (0, 1, 2):
                for hf in halves:
                    ref = rx.at[side, cc, zq, :, rows_of(hf)]
                    pltpu.make_async_copy(ref, ref, x_r.at[side, cc, zq, hf]).wait()
            if cc is c:
                total = psend[x // 2, 4 * (x % 2) + zq, pl.ds(2 * c, 2), rows].astype(F32)
            else:
                total = rx[2, cc, zq, :, rows].astype(F32)
            for side in (0, 1):
                total = total + rx[side, cc, zq, :, rows].astype(F32)

            @pl.when(zq // 2 == yl)
            def _():
                keep[e, cc, :, rows] = total

            @pl.when(zq // 2 != yl)
            def _():
                ysend[e, cc, :, rows] = total.astype(BF16)
                for hf in halves:
                    y_copy(e, cc, hf).start()

    def add_y(i):
        zq = ranked(i)
        e = zq % 2

        @pl.when(zq // 2 == yl)
        def _():
            for hf in (0, 1):
                for cc in (0, 1):
                    y_copy(e, cc, hf).wait_recv()
                    rows = pl.ds(pl.multiple_of(e * 2 * QD + cc * QD + hf * HALF, HALF), HALF)
                    part = slice(hf * HALF, (hf + 1) * HALF)
                    for half in (0, 1):
                        out_buf[rows, half * 256 : (half + 1) * 256] = (
                            keep[e, cc, half, part] + ry[e, cc, half, part].astype(F32)
                        ).astype(BF16)

    def proj_group(k, carry):
        for i in range(7):

            @pl.when(k == i)
            def _():
                before(ga, i, False)


        project(group_z(k), (0, 1))
        for i in range(1, 7):

            @pl.when(k == i)
            def _():
                relay_x(group_z(i - 1), (0, 1))

        return carry

    lax.fori_loop(0, 7, proj_group, 0)
    last = group_z(7)
    ga.forward((0, 1), 4)
    project(last, (0,))
    relay_x(group_z(6), (0, 1))
    ga.forward((3,), 4)
    project(last, (1,))
    relay_x(last, (0,))
    relay_x(last, (1,))
    for i in (0, 1, 2):
        add_x(i, (0, 1))
    for hf in (0, 1):
        add_x(3, (hf,))
    for i in range(4):
        add_y(i)
    proj_out = pltpu.make_async_copy(out_buf, out_hbm, out_sem.at[1])
    proj_out.start()

    for e in (0, 1):
        for cc in (0, 1):
            for hf in (0, 1):
                y_copy(e, cc, hf).wait_send()

    def x_done(zo, carry):
        @pl.when(zo // 4 == x % 2)
        def _():
            for hf in (0, 1):
                to_relay(zo, hf).wait_send()
                to_self(zo, hf).wait_send()

        @pl.when(zo // 4 != x % 2)
        def _():
            for hf in (0, 1):
                for up in (False, True):
                    for other in (0, 1):
                        to_owner(zo, hf, up, other).wait_send()

        return carry

    lax.fori_loop(0, NZ, x_done, 0)
    gk.finish()
    ga.finish()
    att_out.wait()
    proj_out.wait()


def per_device(queries, new_keys, new_values, segment_ids, cache_keys, cache_values, cache_lengths, o_weight):
    any_ = pl.BlockSpec(memory_space=pl.ANY)
    vmem = pl.BlockSpec(memory_space=pltpu.VMEM)
    smem = pl.BlockSpec(memory_space=pltpu.SMEM)
    dma = pltpu.SemaphoreType.DMA
    att, out = pl.pallas_call(
        kernel,
        out_shape=(
            jax.ShapeDtypeStruct((ROWS, HD), BF16),
            jax.ShapeDtypeStruct((4 * QD, 512), BF16),
        ),
        in_specs=[any_, any_, any_, vmem, any_, any_, smem, any_],
        out_specs=(any_, any_),
        scratch_shapes=[
            pltpu.VMEM((2, 2, NZ, PKT, HD), BF16),
            pltpu.VMEM((ROWS, HD), BF16),
            pltpu.VMEM((ROWS, HD), F32),
            pltpu.VMEM((ROWS, HD), F32),
            pltpu.VMEM((ROWS, 2 * HD), F32),
            pltpu.VMEM((2, RCHUNK, 5 * CD), F32),
            pltpu.VMEM((2, RCHUNK, HD), F32),
            pltpu.VMEM((5 * CD, 2 * HD), BF16),
            pltpu.VMEM((4, HEADS * HD, 256), BF16),
            pltpu.VMEM((2, NZ, PAIRS, QD, 256), BF16),
            pltpu.VMEM((ROWS, HD), F32),
            pltpu.VMEM((ROWS, HD), BF16),
            pltpu.VMEM((2, NZ, 4, QD, 256), BF16),
            pltpu.VMEM((4, 2, 4, HALF, 256), BF16),
            pltpu.VMEM((3, 2, 4, 2, QD, 256), BF16),
            pltpu.VMEM((2, 2, 2, QD, 256), F32),
            pltpu.VMEM((2, 2, 2, QD, 256), BF16),
            pltpu.VMEM((2, 2, 2, QD, 256), BF16),
            pltpu.VMEM((4 * QD, 512), BF16),
            dma((5,)), dma((2,)), dma((2,)),
            dma((2, 4, 3)), dma((2, 4, 3)), dma((10,)), dma((10,)), dma((4, 9)), dma((4, 9)),
            dma((2, 4, 4)), dma((2, 4, 4)), dma((10,)), dma((10,)),
            dma((NZ, 2, 4)), dma((3, 2, 4, 2)), dma((4, 2)), dma((2, 2, 2)), dma((2, 2, 2)), dma((2,)), dma((2,)),
        ],
        compiler_params=pltpu.CompilerParams(
            collective_id=0, has_side_effects=True, vmem_limit_bytes=56 << 20
        ),
    )(
        queries.reshape(ROWS, HD),
        new_keys.reshape(QD, HD),
        new_values.reshape(QD, HD),
        segment_ids.reshape(1, QD),
        cache_keys.reshape(CD, HD),
        cache_values.reshape(CD, HD),
        cache_lengths,
        o_weight,
    )
    return att.reshape(QD, HEADS, HD), out


def solution(mesh):
    return jax.shard_map(
        per_device,
        mesh=mesh,
        in_specs=(
            P("blk", "head", None),
            P("blk", "head", None),
            P("blk", "head", None),
            P("blk"),
            P("blk", "head", None),
            P("blk", "head", None),
            P("blk"),
            P("head", "blk"),
        ),
        out_specs=(P("blk", "head", None), P("head", "blk")),
        check_vma=False,
    )
```

```python
import functools
import math

import jax
import jax.numpy as jnp
from jax import lax
from jax.experimental import pallas as pl
from jax.experimental.pallas import tpu as pltpu
from jax.sharding import PartitionSpec as P

MESH = pl.DeviceIdType.MESH
F32 = jnp.float32
BF16 = jnp.bfloat16

QD = 64
CD = 256
HEADS = 16
HD = 128
ROWS = QD * HEADS
NZ = 8
KN0, VN0, META0, PKT = 2 * CD, 2 * CD + QD, 2 * CD + 2 * QD, 2 * CD + 2 * QD + 16
HALF = QD // 2
PAIRS = HEADS // 2
LOW = -1e30
SCALE = math.log2(math.e) / math.sqrt(HD)

KP = 336
KQ_MID = 496
AP = 4
AQ_MID = 6

RCHUNK = 512


def kernel(
    q_hbm, kn_hbm, vn_hbm, seg_ref, kc_hbm, vc_hbm, len_ref, w_hbm,
    att_hbm, out_hbm,
    kv, q_buf, segq, m_buf, acc, sc, m_next, vb, w_buf, abuf, att_f32, att_bf, psend, relay, rx, keep, ysend, ry, out_buf,
    in_sem, w_sem, out_sem,
    kz_s, kz_r, ky_s, ky_r, kb_s, kb_r,
    az_s, az_r, ay_s, ay_r,
    x_s, x_r, r_r, f_s, f_r, wx_s, wx_r,
):
    b = lax.axis_index("blk")
    h = lax.axis_index("head")
    yh, z, c = b // 16, (b // 2) % NZ, b % 2
    x, yl = h // 2, h % 2
    oy, oc = 1 - yh, 1 - c

    def dev(yh_, z_, c_, x_, yl_):
        return {"blk": yh_ * 16 + z_ * 2 + c_, "head": x_ * 2 + yl_}

    right = dev(yh, (z + 1) % NZ, c, x, yl)
    left = dev(yh, (z + NZ - 1) % NZ, c, x, yl)
    across = dev(oy, z, c, x, yl)
    sibling = dev(yh, z, oc, x, yl)
    beside = dev(yh, z, c, x, 1 - yl)
    ring = (right, left)

    def rdma(src, dst, ss, rs, to):
        return pltpu.make_async_remote_copy(
            src_ref=src, dst_ref=dst, send_sem=ss, recv_sem=rs, device_id=to, device_id_type=MESH
        )

    barrier = pltpu.get_barrier_semaphore()
    partners = [right, left, across, sibling, beside]
    for dx in (1, 3):
        for cc in (0, 1):
            partners.append(dev(yh, z, cc, (x + dx) % 4, yl))
    for to in partners:
        pl.semaphore_signal(barrier, inc=1, device_id=to, device_id_type=MESH)

    mine = kv.at[c, yh, z]
    loads = [
        pltpu.make_async_copy(kc_hbm, mine.at[pl.ds(0, CD)], in_sem.at[0]),
        pltpu.make_async_copy(vc_hbm, mine.at[pl.ds(CD, CD)], in_sem.at[1]),
        pltpu.make_async_copy(kn_hbm, mine.at[pl.ds(KN0, QD)], in_sem.at[2]),
        pltpu.make_async_copy(vn_hbm, mine.at[pl.ds(VN0, QD)], in_sem.at[3]),
        pltpu.make_async_copy(q_hbm, q_buf, in_sem.at[4]),
    ]
    for cp in loads:
        cp.start()

    length = len_ref[0]
    seg_row = seg_ref[...].astype(F32)
    seg_row = jnp.concatenate([seg_row, seg_row], axis=1)
    for cp in loads[:4]:
        cp.wait()
    shown = lax.broadcasted_iota(jnp.int32, (CD, HD), 0) < length
    keys = kv[c, yh, z, 0:CD, :].astype(F32)
    kv[c, yh, z, 0:CD, :] = jnp.where(shown, keys, keys[0:1, :]).astype(BF16)
    values = kv[c, yh, z, CD : 2 * CD, :].astype(F32)
    kv[c, yh, z, CD : 2 * CD, :] = jnp.where(shown, values, 0.0).astype(BF16)
    top = lax.broadcasted_iota(jnp.int32, (16, HD), 0) < 8
    kv[c, yh, z, META0:PKT, :] = jnp.where(
        top, jnp.broadcast_to(seg_row, (16, HD)), length.astype(F32)
    ).astype(BF16)

    pl.semaphore_wait(barrier, len(partners))

    class Gather:
        def __init__(self, slot, p, qs, qa, qb, zs, zr, ys, yr, sib=None, tail=None):
            self.slot, self.p, self.q, self.qa, self.qb = slot, p, qs, qa, qb
            self.zs, self.zr, self.ys, self.yr, self.sib = zs, zr, ys, yr, sib
            self.tail = tail
            self.sent = []

        def go(self, copy):
            copy().start()
            self.sent.append(copy)

        def z_of(self, d, s):
            return (z + NZ - s) % NZ if d == 0 else (z + s) % NZ

        def part(self, kind, d, s):
            if kind == 3:
                return self.tail[1] if self.tail and s == 4 else None
            if kind < 2:
                if s == 4 and kind != d:
                    return None
                return self.tail[0] if self.tail and s == 4 else self.p
            if s == 4:
                return self.qa if d == 0 else self.qb
            return self.q

        def view(self, kind, d, s):
            return self.slot(self.plane(kind, d), self.z_of(d, s), self.part(kind, d, s))

        def plane(self, kind, d):
            return oy if kind == 1 or (kind == 3 and d == 1) else yh

        def z_send(self, kind, d, s):
            if self.part(kind, d, s) is None:
                return

            def copy():
                ref = self.slot(self.plane(kind, d), self.z_of(d, s - 1), self.part(kind, d, s))
                return rdma(ref, ref, self.zs.at[d, s - 1, kind], self.zr.at[d, s - 1, kind], ring[d])

            self.go(copy)

        def z_wait(self, kind, d, s):
            if self.part(kind, d, s) is None:
                return
            ref = self.view(kind, d, s)
            rdma(ref, ref, self.zs.at[d, s - 1, kind], self.zr.at[d, s - 1, kind], ring[d]).wait_recv()

        def code(self, d, s):
            return 0 if s == 0 else (1 + d * 3 + s - 1 if s < 4 else 7 + d)

        def y_piece(self, d, s):
            return self.q if s < 4 else (self.qa if d == 0 else self.qb)

        def y_send(self, d, s):
            def copy():
                k = self.code(d, s)
                ref = self.slot(yh, self.z_of(d, s), self.y_piece(d, s))
                return rdma(ref, ref, self.ys.at[k], self.yr.at[k], across)

            self.go(copy)

        def y_wait(self, d, s):
            k = self.code(d, s)
            ref = self.slot(oy, self.z_of(d, s), self.y_piece(d, s))
            rdma(ref, ref, self.ys.at[k], self.yr.at[k], across).wait_recv()

        def yp_send(self):
            def copy():
                ref = self.slot(yh, z, self.p)
                return rdma(ref, ref, self.ys.at[9], self.yr.at[9], across)

            self.go(copy)

        def yp_wait(self):
            ref = self.slot(oy, z, self.p)
            rdma(ref, ref, self.ys.at[9], self.yr.at[9], across).wait_recv()

        def b_ref(self, kind, d, s, core):
            pc = self.p if kind < 2 else self.y_piece(d, s)
            return kv.at[core, oy if kind % 2 else yh, self.z_of(d, s), pl.ds(pc[0], pc[1])]

        def b_send(self, kind, d, s):
            if self.sib is None:
                return
            if kind < 2 and s > 0 and self.part(kind, d, s) is None:
                return

            def copy():
                k = self.code(d, s)
                ref = self.b_ref(kind, d, s, c)
                return rdma(ref, ref, self.sib[0].at[kind, k], self.sib[1].at[kind, k], sibling)

            self.go(copy)

        def b_wait(self, d, s):
            for kind in range(4):
                if kind < 2 and s > 0 and self.part(kind, d, s) is None:
                    continue
                k = self.code(d, s)
                ref = self.b_ref(kind, d, s, oc)
                rdma(ref, ref, self.sib[0].at[kind, k], self.sib[1].at[kind, k], sibling).wait_recv()

        def open(self):
            self.yp_send()
            for kind in (2, 0):
                for d in (0, 1):
                    self.z_send(kind, d, 1)
                if kind == 2:
                    self.y_send(0, 0)
                self.b_send(kind, 0, 0)

        def middle(self):
            self.yp_wait()
            for d in (0, 1):
                self.z_send(1, d, 1)
            self.b_send(1, 0, 0)

        def forward(self, kinds, s):
            for kind in kinds:
                for d in (0, 1):
                    if self.part(kind, d, s) is None:
                        continue
                    self.z_wait(kind, d, s)
                    if s < 4:
                        self.z_send(kind, d, s + 1)
                    if s == 3 and kind == d:
                        self.z_send(3, d, 4)
                    if kind == 2:
                        self.y_send(d, s)
                    self.b_send(kind, d, s)

        def late(self, s):
            for d in (0, 1) if s > 0 else (0,):
                self.y_wait(d, s)
                self.b_send(3, d, s)

        def finish(self):
            for copy in self.sent:
                copy().wait_send()

    def kv_slot(y_, z_, pc):
        return kv.at[c, y_, z_, pl.ds(pc[0], pc[1])]

    gk = Gather(
        kv_slot, (0, KP), (KP, PKT - KP), (KP, KQ_MID - KP), (KQ_MID, PKT - KQ_MID),
        kz_s, kz_r, ky_s, ky_r, (kb_s, kb_r),
    )
    gk.open()

    cols = jnp.broadcast_to(seg_row, (HD, HD)).T[0:QD, :]
    segq[...] = jnp.broadcast_to(cols[:, None, :], (QD, HEADS, HD)).reshape(ROWS, HD)
    m_buf[...] = jnp.full((ROWS, HD), LOW, F32)
    acc[...] = jnp.zeros((ROWS, 2 * HD), F32)
    loads[4].wait()

    lane = lax.broadcasted_iota(jnp.int32, (1, CD), 1)
    lane_blk = (lane // 128) * 16 + (lane // 64) % 2
    order = [(0, 0), (0, 1), (1, 0), (1, 1)]

    def attend(zo):
        key_blk = lane_blk + zo * 2
        seg0 = [kv[c_, y_, zo, META0:PKT, :][0:1, :].astype(F32) for y_, c_ in order]
        lens = [kv[c_, y_, zo, META0:PKT, :][8:9, :].astype(F32) for y_, c_ in order]
        low = lax.broadcasted_iota(jnp.int32, (1, HD), 1) < QD
        seg_k = jnp.concatenate([jnp.where(low, seg0[0], seg0[1]), jnp.where(low, seg0[2], seg0[3])], axis=1)
        key_row = key_blk * QD + lane % QD
        slot = lax.broadcasted_iota(jnp.int32, (CD, HD), 0).astype(F32)
        for i, (y_, c_) in enumerate(order):
            vb[i * CD : (i + 1) * CD, 0:HD] = kv[c_, y_, zo, CD : 2 * CD, :]
            vb[i * CD : (i + 1) * CD, HD : 2 * HD] = jnp.where(slot < lens[i], 1.0, 0.0).astype(BF16)
            vb[4 * CD + i * QD : 4 * CD + (i + 1) * QD, 0:HD] = kv[c_, y_, zo, VN0 : VN0 + QD, :]
        vb[4 * CD : 5 * CD, HD : 2 * HD] = jnp.ones((CD, HD), BF16)

        def scores(r):
            rows = pl.ds(r * RCHUNK, RCHUNK)
            q = q_buf[rows, :]
            tops = None
            for i in range(5):
                if i < 4:
                    y_, c_ = order[i]
                    keys = kv[c_, y_, zo, 0:CD, :]
                else:
                    keys = jnp.concatenate([kv[c_, y_, zo, KN0 : KN0 + QD, :] for y_, c_ in order], axis=0)
                s = lax.dot_general(q, keys, (((1,), (1,)), ((), ())), preferred_element_type=F32)
                if i == 4:
                    sq = segq[rows, :]
                    sees = jnp.concatenate([sq, sq], axis=1) == seg_k
                    tok = (lax.broadcasted_iota(jnp.int32, (RCHUNK, CD), 0) + r * RCHUNK) // HEADS
                    s = jnp.where(sees & (key_row <= tok + b * QD), s, LOW)
                sc[r % 2, :, i * CD : (i + 1) * CD] = s
                top = jnp.maximum(s[:, 0:HD], s[:, HD : 2 * HD])
                tops = top if tops is None else jnp.maximum(tops, top)
            m_next[r % 2] = jnp.maximum(m_buf[rows, :], jnp.max(tops, axis=1, keepdims=True))

        def weigh(r):
            rows = pl.ds(r * RCHUNK, RCHUNK)
            m_new = m_next[r % 2]
            shrink = jnp.exp2((m_buf[rows, :] - m_new) * SCALE)
            m_buf[rows, :] = m_new
            base = m_new * SCALE
            w = jnp.concatenate(
                [
                    jnp.exp2(sc[r % 2, :, i * HD : (i + 1) * HD] * SCALE - base).astype(BF16)
                    for i in range(10)
                ],
                axis=1,
            )
            acc[rows, :] = acc[rows, :] * jnp.concatenate([shrink, shrink], axis=1) + jnp.dot(
                w, vb[...], preferred_element_type=F32
            )

        n = ROWS // RCHUNK
        scores(0)
        for r in range(n):
            if r + 1 < n:
                scores(r + 1)
            weigh(r)

    def group_z(k):
        s = (k + 1) // 2
        return (z + (1 - 2 * (k % 2)) * s + NZ) % NZ

    def arrived(g, k):
        s = (k + 1) // 2
        g.b_wait(0 if s == 0 else 1 - k % 2, s)
        if s == 4:
            g.b_wait(1, s)

    def before(g, k):
        q_at = {0: 1, 1: 2, 2: 3, 4: 4}
        if k in q_at:
            g.forward((2,), q_at[k])
        if k == 0:
            g.middle()
            g.late(0)
            return
        s = (k + 1) // 2
        if k % 2:
            g.forward((0, 1), s)
        if k in (1, 3, 5, 6):
            g.late((k + 2) // 2)

    def weights(i):
        half = w_hbm.at[:, pl.ds(i * 256, 256)]
        slot = w_buf.at[2 * c + i]
        here = pltpu.make_async_copy(half, slot, w_sem.at[i])
        return here, rdma(half, slot, wx_s.at[i], wx_r.at[i], sibling)

    def kv_group(k, carry):
        for i in range(9):

            @pl.when(k == i)
            def _():
                if i < 8:
                    before(gk, i)
                if i > 0:
                    arrived(gk, i - 1)
                if i in (2, 3):
                    for cp in weights(i - 2):
                        cp.start()

        @pl.when(k > 0)
        def _():
            attend(group_z(k - 1))

        return carry

    lax.fori_loop(0, 9, kv_group, 0)

    def finish_rows(r, carry):
        rows = pl.ds(pl.multiple_of(r * RCHUNK, RCHUNK), RCHUNK)
        o = acc[rows, 0:HD] / acc[rows, HD : 2 * HD]
        att_f32[rows, :] = o
        att_bf[rows, :] = o.astype(BF16)
        return carry

    lax.fori_loop(0, ROWS // RCHUNK, finish_rows, 0)
    for i in range(HEADS):
        abuf[yh, z, i // 2, :, (i % 2) * HD : (i % 2 + 1) * HD] = att_f32[
            pl.ds(i, QD, stride=HEADS), :
        ].astype(BF16)

    ga = Gather(
        lambda y_, z_, pc: abuf.at[y_, z_, pl.ds(pc[0], pc[1]), pl.ds(pc[2] if len(pc) > 2 else 0, QD // 2 if len(pc) > 2 else QD)],
        (0, AP), (AP, PAIRS - AP), (AP, AQ_MID - AP), (AQ_MID, PAIRS - AQ_MID),
        az_s, az_r, ay_s, ay_r, None, ((0, AP, 0), (0, AP, QD // 2)),
    )
    ga.open()
    att_out = pltpu.make_async_copy(att_bf, att_hbm, out_sem.at[0])
    att_out.start()
    for i in (0, 1):
        for cp in weights(i):
            cp.wait()

    def rows_of(hf):
        return pl.ds(hf * HALF, HALF)

    def to_self(zo, hf):
        return rdma(
            psend.at[x // 2, zo, pl.ds(2 * oc, 2), rows_of(hf)],
            rx.at[2, c, zo % 4, :, rows_of(hf)],
            x_s.at[zo, hf, 0], x_r.at[2, c, zo % 4, hf], sibling,
        )

    def to_relay(zo, hf):
        via = (x + (1 if hf == 0 else 3)) % 4
        return rdma(
            psend.at[1 - x // 2, zo, :, rows_of(hf)],
            relay.at[zo % 4, hf],
            x_s.at[zo, hf, 1], r_r.at[zo % 4, hf], dev(yh, z, c, via, yl),
        )

    def to_owner(zo, hf, up, other):
        owner = (x + (1 if up else 3)) % 4
        to_c = oc if other else c
        relayed = (hf == 0) == up
        return rdma(
            psend.at[owner // 2, zo, pl.ds(2 * to_c, 2), rows_of(hf)],
            rx.at[0 if up else 1, c, zo % 4, :, rows_of(hf)],
            x_s.at[zo, hf, 2 * relayed + other], x_r.at[0 if up else 1, c, zo % 4, hf],
            dev(yh, z, to_c, owner, yl),
        )

    def send_x(zo, halves):
        @pl.when(zo // 4 == x % 2)
        def _():
            for hf in halves:
                to_relay(zo, hf).start()
                to_self(zo, hf).start()

        @pl.when(zo // 4 != x % 2)
        def _():
            for hf in halves:
                for other in (0, 1):
                    to_owner(zo, hf, hf == 1, other).start()

    def relay_x(zo, halves):
        @pl.when(zo // 4 != x % 2)
        def _():
            for hf in halves:
                to_relay(zo, hf).wait_recv()
                y_ = ((x + (1 if hf == 0 else 3)) % 4) // 2
                mine = psend.at[y_, zo]
                rows = slice(hf * HALF, (hf + 1) * HALF)
                mine[:, rows] = (mine[:, rows].astype(F32) + relay[zo % 4, hf].astype(F32)).astype(BF16)
                for other in (0, 1):
                    to_owner(zo, hf, hf == 0, other).start()

    def project(zo, halves):
        first, count = halves[0] * HALF, len(halves) * HALF

        def body(n, carry):
            total = jnp.zeros((2 * count, 256), F32)
            for j in range(PAIRS):
                lhs = jnp.concatenate(
                    [abuf[yh, zo, j, first : first + count], abuf[oy, zo, j, first : first + count]], axis=0
                )
                total = total + jnp.dot(
                    lhs, w_buf[n, j * 256 : (j + 1) * 256, :], preferred_element_type=F32
                )
            psend[yh, zo, n, first : first + count] = total[0:count].astype(BF16)
            psend[oy, zo, n, first : first + count] = total[count : 2 * count].astype(BF16)
            return carry

        lax.fori_loop(0, 4, body, 0)
        send_x(zo, halves)

    u = (z - 4 * (x % 2) + NZ) % NZ
    power = (1 + 3 * (u % 2)) * (1 + 15 * ((u // 2) % 2)) * (1 + 255 * (u // 4))

    def ranked(i):
        table = ((0, 1, 2, 3, 3, 3, 0, 0), (1, 0, 1, 2, 2, 2, 3, 1), (2, 2, 3, 1, 1, 0, 1, 2), (3, 3, 0, 0, 0, 1, 2, 3))[i]
        return (sum(v * 4**n for n, v in enumerate(table)) // power) % 4

    def y_copy(e, cc, hf):
        rows = pl.ds(hf * HALF, HALF)
        return rdma(
            ysend.at[e, cc, :, rows], ry.at[e, cc, :, rows], f_s.at[e, cc, hf], f_r.at[e, cc, hf], beside
        )

    def add_x(i, halves):
        zq = ranked(i)
        e = zq % 2
        first, count = halves[0] * HALF, len(halves) * HALF
        rows = slice(first, first + count)
        for cc in (c, oc):
            for side in (0, 1) if cc is c else (0, 1, 2):
                for hf in halves:
                    ref = rx.at[side, cc, zq, :, rows_of(hf)]
                    pltpu.make_async_copy(ref, ref, x_r.at[side, cc, zq, hf]).wait()
            if cc is c:
                total = psend[x // 2, 4 * (x % 2) + zq, pl.ds(2 * c, 2), rows].astype(F32)
            else:
                total = rx[2, cc, zq, :, rows].astype(F32)
            for side in (0, 1):
                total = total + rx[side, cc, zq, :, rows].astype(F32)

            @pl.when(zq // 2 == yl)
            def _():
                keep[e, cc, :, rows] = total

            @pl.when(zq // 2 != yl)
            def _():
                ysend[e, cc, :, rows] = total.astype(BF16)
                for hf in halves:
                    y_copy(e, cc, hf).start()

    def add_y(i):
        zq = ranked(i)
        e = zq % 2

        @pl.when(zq // 2 == yl)
        def _():
            for hf in (0, 1):
                for cc in (0, 1):
                    y_copy(e, cc, hf).wait_recv()
                    rows = pl.ds(pl.multiple_of(e * 2 * QD + cc * QD + hf * HALF, HALF), HALF)
                    part = slice(hf * HALF, (hf + 1) * HALF)
                    for half in (0, 1):
                        out_buf[rows, half * 256 : (half + 1) * 256] = (
                            keep[e, cc, half, part] + ry[e, cc, half, part].astype(F32)
                        ).astype(BF16)

    def proj_group(k, carry):
        for i in range(7):

            @pl.when(k == i)
            def _():
                before(ga, i)


        project(group_z(k), (0, 1))
        for i in range(1, 7):

            @pl.when(k == i)
            def _():
                relay_x(group_z(i - 1), (0, 1))

        return carry

    lax.fori_loop(0, 7, proj_group, 0)
    last = group_z(7)
    ga.forward((0, 1), 4)
    project(last, (0,))
    add_x(0, (0, 1))
    relay_x(group_z(6), (0, 1))
    ga.forward((3,), 4)
    project(last, (1,))
    relay_x(last, (0,))
    add_x(1, (0, 1))
    relay_x(last, (1,))
    add_x(2, (0, 1))
    for hf in (0, 1):
        add_x(3, (hf,))
    for i in range(4):
        add_y(i)
    proj_out = pltpu.make_async_copy(out_buf, out_hbm, out_sem.at[1])
    proj_out.start()

    for e in (0, 1):
        for cc in (0, 1):
            for hf in (0, 1):
                y_copy(e, cc, hf).wait_send()

    def x_done(zo, carry):
        @pl.when(zo // 4 == x % 2)
        def _():
            for hf in (0, 1):
                to_relay(zo, hf).wait_send()
                to_self(zo, hf).wait_send()

        @pl.when(zo // 4 != x % 2)
        def _():
            for hf in (0, 1):
                for up in (False, True):
                    for other in (0, 1):
                        to_owner(zo, hf, up, other).wait_send()

        return carry

    lax.fori_loop(0, NZ, x_done, 0)
    gk.finish()
    ga.finish()
    att_out.wait()
    proj_out.wait()


def per_device(queries, new_keys, new_values, segment_ids, cache_keys, cache_values, cache_lengths, o_weight):
    any_ = pl.BlockSpec(memory_space=pl.ANY)
    vmem = pl.BlockSpec(memory_space=pltpu.VMEM)
    smem = pl.BlockSpec(memory_space=pltpu.SMEM)
    dma = pltpu.SemaphoreType.DMA
    att, out = pl.pallas_call(
        kernel,
        out_shape=(
            jax.ShapeDtypeStruct((ROWS, HD), BF16),
            jax.ShapeDtypeStruct((4 * QD, 512), BF16),
        ),
        in_specs=[any_, any_, any_, vmem, any_, any_, smem, any_],
        out_specs=(any_, any_),
        scratch_shapes=[
            pltpu.VMEM((2, 2, NZ, PKT, HD), BF16),
            pltpu.VMEM((ROWS, HD), BF16),
            pltpu.VMEM((ROWS, HD), F32),
            pltpu.VMEM((ROWS, HD), F32),
            pltpu.VMEM((ROWS, 2 * HD), F32),
            pltpu.VMEM((2, RCHUNK, 5 * CD), F32),
            pltpu.VMEM((2, RCHUNK, HD), F32),
            pltpu.VMEM((5 * CD, 2 * HD), BF16),
            pltpu.VMEM((4, HEADS * HD, 256), BF16),
            pltpu.VMEM((2, NZ, PAIRS, QD, 256), BF16),
            pltpu.VMEM((ROWS, HD), F32),
            pltpu.VMEM((ROWS, HD), BF16),
            pltpu.VMEM((2, NZ, 4, QD, 256), BF16),
            pltpu.VMEM((4, 2, 4, HALF, 256), BF16),
            pltpu.VMEM((3, 2, 4, 2, QD, 256), BF16),
            pltpu.VMEM((2, 2, 2, QD, 256), F32),
            pltpu.VMEM((2, 2, 2, QD, 256), BF16),
            pltpu.VMEM((2, 2, 2, QD, 256), BF16),
            pltpu.VMEM((4 * QD, 512), BF16),
            dma((5,)), dma((2,)), dma((2,)),
            dma((2, 4, 3)), dma((2, 4, 3)), dma((10,)), dma((10,)), dma((4, 9)), dma((4, 9)),
            dma((2, 4, 4)), dma((2, 4, 4)), dma((10,)), dma((10,)),
            dma((NZ, 2, 4)), dma((3, 2, 4, 2)), dma((4, 2)), dma((2, 2, 2)), dma((2, 2, 2)), dma((2,)), dma((2,)),
        ],
        compiler_params=pltpu.CompilerParams(
            collective_id=0, has_side_effects=True, vmem_limit_bytes=56 << 20
        ),
    )(
        queries.reshape(ROWS, HD),
        new_keys.reshape(QD, HD),
        new_values.reshape(QD, HD),
        segment_ids.reshape(1, QD),
        cache_keys.reshape(CD, HD),
        cache_values.reshape(CD, HD),
        cache_lengths,
        o_weight,
    )
    return att.reshape(QD, HEADS, HD), out


def solution(mesh):
    return jax.shard_map(
        per_device,
        mesh=mesh,
        in_specs=(
            P("blk", "head", None),
            P("blk", "head", None),
            P("blk", "head", None),
            P("blk"),
            P("blk", "head", None),
            P("blk", "head", None),
            P("blk"),
            P("head", "blk"),
        ),
        out_specs=(P("blk", "head", None), P("head", "blk")),
        check_vma=False,
    )
```

```python
import functools
import math

import jax
import jax.numpy as jnp
from jax import lax
from jax.experimental import pallas as pl
from jax.experimental.pallas import tpu as pltpu
from jax.sharding import PartitionSpec as P

MESH = pl.DeviceIdType.MESH
F32 = jnp.float32
BF16 = jnp.bfloat16

QD = 64
CD = 256
HEADS = 16
HD = 128
ROWS = QD * HEADS
NZ = 8
KN0, VN0, META0, PKT = 2 * CD, 2 * CD + QD, 2 * CD + 2 * QD, 2 * CD + 2 * QD + 16
HALF = QD // 2
PAIRS = HEADS // 2
LOW = -1e30
SCALE = math.log2(math.e) / math.sqrt(HD)

KP = 336
KQ_MID = 496
AP = 4
AQ_MID = 6

RCHUNK = 512


def kernel(
    q_hbm, kn_hbm, vn_hbm, seg_ref, kc_hbm, vc_hbm, len_ref, w_hbm,
    att_hbm, out_hbm,
    kv, q_buf, segq, m_buf, acc, sc, m_next, vb, w_buf, abuf, att_f32, att_bf, psend, relay, rx, keep, ysend, ry, out_buf,
    in_sem, w_sem, out_sem,
    kz_s, kz_r, ky_s, ky_r, kb_s, kb_r,
    az_s, az_r, ay_s, ay_r,
    x_s, x_r, r_r, f_s, f_r, wx_s, wx_r,
):
    b = lax.axis_index("blk")
    h = lax.axis_index("head")
    yh, z, c = b // 16, (b // 2) % NZ, b % 2
    x, yl = h // 2, h % 2
    oy, oc = 1 - yh, 1 - c

    def dev(yh_, z_, c_, x_, yl_):
        return {"blk": yh_ * 16 + z_ * 2 + c_, "head": x_ * 2 + yl_}

    right = dev(yh, (z + 1) % NZ, c, x, yl)
    left = dev(yh, (z + NZ - 1) % NZ, c, x, yl)
    across = dev(oy, z, c, x, yl)
    sibling = dev(yh, z, oc, x, yl)
    beside = dev(yh, z, c, x, 1 - yl)
    ring = (right, left)

    def rdma(src, dst, ss, rs, to):
        return pltpu.make_async_remote_copy(
            src_ref=src, dst_ref=dst, send_sem=ss, recv_sem=rs, device_id=to, device_id_type=MESH
        )

    barrier = pltpu.get_barrier_semaphore()
    partners = [right, left, across, sibling, beside]
    for dx in (1, 3):
        for cc in (0, 1):
            partners.append(dev(yh, z, cc, (x + dx) % 4, yl))
    for to in partners:
        pl.semaphore_signal(barrier, inc=1, device_id=to, device_id_type=MESH)

    mine = kv.at[c, yh, z]
    loads = [
        pltpu.make_async_copy(kc_hbm, mine.at[pl.ds(0, CD)], in_sem.at[0]),
        pltpu.make_async_copy(vc_hbm, mine.at[pl.ds(CD, CD)], in_sem.at[1]),
        pltpu.make_async_copy(kn_hbm, mine.at[pl.ds(KN0, QD)], in_sem.at[2]),
        pltpu.make_async_copy(vn_hbm, mine.at[pl.ds(VN0, QD)], in_sem.at[3]),
        pltpu.make_async_copy(q_hbm, q_buf, in_sem.at[4]),
    ]
    for cp in loads:
        cp.start()

    length = len_ref[0]
    seg_row = seg_ref[...].astype(F32)
    seg_row = jnp.concatenate([seg_row, seg_row], axis=1)
    for cp in loads[:4]:
        cp.wait()
    shown = lax.broadcasted_iota(jnp.int32, (CD, HD), 0) < length
    keys = kv[c, yh, z, 0:CD, :].astype(F32)
    kv[c, yh, z, 0:CD, :] = jnp.where(shown, keys, keys[0:1, :]).astype(BF16)
    values = kv[c, yh, z, CD : 2 * CD, :].astype(F32)
    kv[c, yh, z, CD : 2 * CD, :] = jnp.where(shown, values, 0.0).astype(BF16)
    top = lax.broadcasted_iota(jnp.int32, (16, HD), 0) < 8
    kv[c, yh, z, META0:PKT, :] = jnp.where(
        top, jnp.broadcast_to(seg_row, (16, HD)), length.astype(F32)
    ).astype(BF16)

    pl.semaphore_wait(barrier, len(partners))

    class Gather:
        def __init__(self, slot, p, qs, qa, qb, zs, zr, ys, yr, sib=None, tail=None):
            self.slot, self.p, self.q, self.qa, self.qb = slot, p, qs, qa, qb
            self.zs, self.zr, self.ys, self.yr, self.sib = zs, zr, ys, yr, sib
            self.tail = tail
            self.sent = []

        def go(self, copy):
            copy().start()
            self.sent.append(copy)

        def z_of(self, d, s):
            return (z + NZ - s) % NZ if d == 0 else (z + s) % NZ

        def part(self, kind, d, s):
            if kind == 3:
                return self.tail[1] if self.tail and s == 4 else None
            if kind < 2:
                if s == 4 and kind != d:
                    return None
                return self.tail[0] if self.tail and s == 4 else self.p
            if s == 4:
                return self.qa if d == 0 else self.qb
            return self.q

        def view(self, kind, d, s):
            return self.slot(self.plane(kind, d), self.z_of(d, s), self.part(kind, d, s))

        def plane(self, kind, d):
            return oy if kind == 1 or (kind == 3 and d == 1) else yh

        def z_send(self, kind, d, s):
            if self.part(kind, d, s) is None:
                return

            def copy():
                ref = self.slot(self.plane(kind, d), self.z_of(d, s - 1), self.part(kind, d, s))
                return rdma(ref, ref, self.zs.at[d, s - 1, kind], self.zr.at[d, s - 1, kind], ring[d])

            self.go(copy)

        def z_wait(self, kind, d, s):
            if self.part(kind, d, s) is None:
                return
            ref = self.view(kind, d, s)
            rdma(ref, ref, self.zs.at[d, s - 1, kind], self.zr.at[d, s - 1, kind], ring[d]).wait_recv()

        def code(self, d, s):
            return 0 if s == 0 else (1 + d * 3 + s - 1 if s < 4 else 7 + d)

        def y_piece(self, d, s):
            return self.q if s < 4 else (self.qa if d == 0 else self.qb)

        def y_send(self, d, s):
            def copy():
                k = self.code(d, s)
                ref = self.slot(yh, self.z_of(d, s), self.y_piece(d, s))
                return rdma(ref, ref, self.ys.at[k], self.yr.at[k], across)

            self.go(copy)

        def y_wait(self, d, s):
            k = self.code(d, s)
            ref = self.slot(oy, self.z_of(d, s), self.y_piece(d, s))
            rdma(ref, ref, self.ys.at[k], self.yr.at[k], across).wait_recv()

        def yp_send(self):
            def copy():
                ref = self.slot(yh, z, self.p)
                return rdma(ref, ref, self.ys.at[9], self.yr.at[9], across)

            self.go(copy)

        def yp_wait(self):
            ref = self.slot(oy, z, self.p)
            rdma(ref, ref, self.ys.at[9], self.yr.at[9], across).wait_recv()

        def b_ref(self, kind, d, s, core):
            pc = self.p if kind < 2 else self.y_piece(d, s)
            return kv.at[core, oy if kind % 2 else yh, self.z_of(d, s), pl.ds(pc[0], pc[1])]

        def b_send(self, kind, d, s):
            if self.sib is None:
                return
            if kind < 2 and s > 0 and self.part(kind, d, s) is None:
                return

            def copy():
                k = self.code(d, s)
                ref = self.b_ref(kind, d, s, c)
                return rdma(ref, ref, self.sib[0].at[kind, k], self.sib[1].at[kind, k], sibling)

            self.go(copy)

        def b_wait(self, d, s):
            for kind in range(4):
                if kind < 2 and s > 0 and self.part(kind, d, s) is None:
                    continue
                k = self.code(d, s)
                ref = self.b_ref(kind, d, s, oc)
                rdma(ref, ref, self.sib[0].at[kind, k], self.sib[1].at[kind, k], sibling).wait_recv()

        def open(self):
            self.yp_send()
            for kind in (2, 0):
                for d in (0, 1):
                    self.z_send(kind, d, 1)
                if kind == 2:
                    self.y_send(0, 0)
                self.b_send(kind, 0, 0)

        def middle(self):
            self.yp_wait()
            for d in (0, 1):
                self.z_send(1, d, 1)
            self.b_send(1, 0, 0)

        def forward(self, kinds, s):
            for kind in kinds:
                for d in (0, 1):
                    if self.part(kind, d, s) is None:
                        continue
                    self.z_wait(kind, d, s)
                    if s < 4:
                        self.z_send(kind, d, s + 1)
                    if s == 3 and kind == d:
                        self.z_send(3, d, 4)
                    if kind == 2:
                        self.y_send(d, s)
                    self.b_send(kind, d, s)

        def late(self, s):
            for d in (0, 1) if s > 0 else (0,):
                self.y_wait(d, s)
                self.b_send(3, d, s)

        def finish(self):
            for copy in self.sent:
                copy().wait_send()

    def kv_slot(y_, z_, pc):
        return kv.at[c, y_, z_, pl.ds(pc[0], pc[1])]

    gk = Gather(
        kv_slot, (0, KP), (KP, PKT - KP), (KP, KQ_MID - KP), (KQ_MID, PKT - KQ_MID),
        kz_s, kz_r, ky_s, ky_r, (kb_s, kb_r),
    )
    gk.open()

    cols = jnp.broadcast_to(seg_row, (HD, HD)).T[0:QD, :]
    segq[...] = jnp.broadcast_to(cols[:, None, :], (QD, HEADS, HD)).reshape(ROWS, HD)
    m_buf[...] = jnp.full((ROWS, HD), LOW, F32)
    acc[...] = jnp.zeros((ROWS, 2 * HD), F32)
    loads[4].wait()

    lane = lax.broadcasted_iota(jnp.int32, (1, CD), 1)
    lane_blk = (lane // 128) * 16 + (lane // 64) % 2
    order = [(0, 0), (0, 1), (1, 0), (1, 1)]

    def attend(zo):
        key_blk = lane_blk + zo * 2
        seg0 = [kv[c_, y_, zo, META0:PKT, :][0:1, :].astype(F32) for y_, c_ in order]
        lens = [kv[c_, y_, zo, META0:PKT, :][8:9, :].astype(F32) for y_, c_ in order]
        low = lax.broadcasted_iota(jnp.int32, (1, HD), 1) < QD
        seg_k = jnp.concatenate([jnp.where(low, seg0[0], seg0[1]), jnp.where(low, seg0[2], seg0[3])], axis=1)
        key_row = key_blk * QD + lane % QD
        slot = lax.broadcasted_iota(jnp.int32, (CD, HD), 0).astype(F32)
        for i, (y_, c_) in enumerate(order):
            vb[i * CD : (i + 1) * CD, 0:HD] = kv[c_, y_, zo, CD : 2 * CD, :]
            vb[i * CD : (i + 1) * CD, HD : 2 * HD] = jnp.where(slot < lens[i], 1.0, 0.0).astype(BF16)
            vb[4 * CD + i * QD : 4 * CD + (i + 1) * QD, 0:HD] = kv[c_, y_, zo, VN0 : VN0 + QD, :]
        vb[4 * CD : 5 * CD, HD : 2 * HD] = jnp.ones((CD, HD), BF16)

        def scores(r):
            rows = pl.ds(r * RCHUNK, RCHUNK)
            q = q_buf[rows, :]
            tops = None
            for i in range(5):
                if i < 4:
                    y_, c_ = order[i]
                    keys = kv[c_, y_, zo, 0:CD, :]
                else:
                    keys = jnp.concatenate([kv[c_, y_, zo, KN0 : KN0 + QD, :] for y_, c_ in order], axis=0)
                s = lax.dot_general(q, keys, (((1,), (1,)), ((), ())), preferred_element_type=F32)
                if i == 4:
                    sq = segq[rows, :]
                    sees = jnp.concatenate([sq, sq], axis=1) == seg_k
                    tok = (lax.broadcasted_iota(jnp.int32, (RCHUNK, CD), 0) + r * RCHUNK) // HEADS
                    s = jnp.where(sees & (key_row <= tok + b * QD), s, LOW)
                sc[r % 2, :, i * CD : (i + 1) * CD] = s
                top = jnp.maximum(s[:, 0:HD], s[:, HD : 2 * HD])
                tops = top if tops is None else jnp.maximum(tops, top)
            m_next[r % 2] = jnp.maximum(m_buf[rows, :], jnp.max(tops, axis=1, keepdims=True))

        def weigh(r):
            rows = pl.ds(r * RCHUNK, RCHUNK)
            m_new = m_next[r % 2]
            shrink = jnp.exp2((m_buf[rows, :] - m_new) * SCALE)
            m_buf[rows, :] = m_new
            base = m_new * SCALE
            w = jnp.concatenate(
                [
                    jnp.exp2(sc[r % 2, :, i * HD : (i + 1) * HD] * SCALE - base).astype(BF16)
                    for i in range(10)
                ],
                axis=1,
            )
            acc[rows, :] = acc[rows, :] * jnp.concatenate([shrink, shrink], axis=1) + jnp.dot(
                w, vb[...], preferred_element_type=F32
            )

        n = ROWS // RCHUNK
        scores(0)
        for r in range(n):
            if r + 1 < n:
                scores(r + 1)
            weigh(r)

    def group_z(k):
        s = (k + 1) // 2
        return (z + (1 - 2 * (k % 2)) * s + NZ) % NZ

    def arrived(g, k):
        s = (k + 1) // 2
        g.b_wait(0 if s == 0 else 1 - k % 2, s)
        if s == 4:
            g.b_wait(1, s)

    def before(g, k):
        q_at = {0: 1, 1: 2, 2: 3, 4: 4}
        if k in q_at:
            g.forward((2,), q_at[k])
        if k == 0:
            g.middle()
            g.late(0)
            return
        s = (k + 1) // 2
        if k % 2:
            g.forward((0, 1), s)
        if k in (1, 3, 5, 6):
            g.late((k + 2) // 2)

    def weights(i):
        half = w_hbm.at[:, pl.ds(i * 256, 256)]
        slot = w_buf.at[2 * c + i]
        here = pltpu.make_async_copy(half, slot, w_sem.at[i])
        return here, rdma(half, slot, wx_s.at[i], wx_r.at[i], sibling)

    def kv_group(k, carry):
        for i in range(9):

            @pl.when(k == i)
            def _():
                if i < 8:
                    before(gk, i)
                if i > 0:
                    arrived(gk, i - 1)
                if i in (2, 3):
                    for cp in weights(i - 2):
                        cp.start()

        @pl.when(k > 0)
        def _():
            attend(group_z(k - 1))

        return carry

    lax.fori_loop(0, 9, kv_group, 0)

    def finish_rows(r, carry):
        rows = pl.ds(pl.multiple_of(r * RCHUNK, RCHUNK), RCHUNK)
        o = acc[rows, 0:HD] / acc[rows, HD : 2 * HD]
        att_f32[rows, :] = o
        att_bf[rows, :] = o.astype(BF16)
        return carry

    lax.fori_loop(0, ROWS // RCHUNK, finish_rows, 0)
    for i in range(HEADS):
        abuf[yh, z, i // 2, :, (i % 2) * HD : (i % 2 + 1) * HD] = att_f32[
            pl.ds(i, QD, stride=HEADS), :
        ].astype(BF16)

    ga = Gather(
        lambda y_, z_, pc: abuf.at[y_, z_, pl.ds(pc[0], pc[1]), pl.ds(pc[2] if len(pc) > 2 else 0, QD // 2 if len(pc) > 2 else QD)],
        (0, AP), (AP, PAIRS - AP), (AP, AQ_MID - AP), (AQ_MID, PAIRS - AQ_MID),
        az_s, az_r, ay_s, ay_r, None, ((0, AP, 0), (0, AP, QD // 2)),
    )
    ga.open()
    att_out = pltpu.make_async_copy(att_bf, att_hbm, out_sem.at[0])
    att_out.start()
    for i in (0, 1):
        for cp in weights(i):
            cp.wait()

    def rows_of(hf):
        return pl.ds(hf * HALF, HALF)

    def to_self(zo, hf):
        return rdma(
            psend.at[x // 2, zo, pl.ds(2 * oc, 2), rows_of(hf)],
            rx.at[2, c, zo % 4, :, rows_of(hf)],
            x_s.at[zo, hf, 0], x_r.at[2, c, zo % 4, hf], sibling,
        )

    def to_relay(zo, hf):
        via = (x + (1 if hf == 0 else 3)) % 4
        return rdma(
            psend.at[1 - x // 2, zo, :, rows_of(hf)],
            relay.at[zo % 4, hf],
            x_s.at[zo, hf, 1], r_r.at[zo % 4, hf], dev(yh, z, c, via, yl),
        )

    def to_owner(zo, hf, up, other):
        owner = (x + (1 if up else 3)) % 4
        to_c = oc if other else c
        relayed = (hf == 0) == up
        return rdma(
            psend.at[owner // 2, zo, pl.ds(2 * to_c, 2), rows_of(hf)],
            rx.at[0 if up else 1, c, zo % 4, :, rows_of(hf)],
            x_s.at[zo, hf, 2 * relayed + other], x_r.at[0 if up else 1, c, zo % 4, hf],
            dev(yh, z, to_c, owner, yl),
        )

    def send_x(zo, halves):
        @pl.when(zo // 4 == x % 2)
        def _():
            for hf in halves:
                to_relay(zo, hf).start()
                to_self(zo, hf).start()

        @pl.when(zo // 4 != x % 2)
        def _():
            for hf in halves:
                for other in (0, 1):
                    to_owner(zo, hf, hf == 1, other).start()

    def relay_x(zo, halves):
        @pl.when(zo // 4 != x % 2)
        def _():
            for hf in halves:
                to_relay(zo, hf).wait_recv()
                y_ = ((x + (1 if hf == 0 else 3)) % 4) // 2
                mine = psend.at[y_, zo]
                rows = slice(hf * HALF, (hf + 1) * HALF)
                mine[:, rows] = (mine[:, rows].astype(F32) + relay[zo % 4, hf].astype(F32)).astype(BF16)
                for other in (0, 1):
                    to_owner(zo, hf, hf == 0, other).start()

    def project(zo, halves):
        first, count = halves[0] * HALF, len(halves) * HALF

        def body(n, carry):
            total = jnp.zeros((2 * count, 256), F32)
            for j in range(PAIRS):
                lhs = jnp.concatenate(
                    [abuf[yh, zo, j, first : first + count], abuf[oy, zo, j, first : first + count]], axis=0
                )
                total = total + jnp.dot(
                    lhs, w_buf[n, j * 256 : (j + 1) * 256, :], preferred_element_type=F32
                )
            psend[yh, zo, n, first : first + count] = total[0:count].astype(BF16)
            psend[oy, zo, n, first : first + count] = total[count : 2 * count].astype(BF16)
            return carry

        lax.fori_loop(0, 4, body, 0)
        send_x(zo, halves)

    u = (z - 4 * (x % 2) + NZ) % NZ
    power = (1 + 3 * (u % 2)) * (1 + 15 * ((u // 2) % 2)) * (1 + 255 * (u // 4))

    def ranked(i):
        table = ((0, 1, 2, 3, 3, 3, 0, 0), (1, 0, 1, 2, 2, 2, 3, 1), (2, 2, 3, 1, 1, 0, 1, 2), (3, 3, 0, 0, 0, 1, 2, 3))[i]
        return (sum(v * 4**n for n, v in enumerate(table)) // power) % 4

    def y_copy(e, cc, hf):
        rows = pl.ds(hf * HALF, HALF)
        return rdma(
            ysend.at[e, cc, :, rows], ry.at[e, cc, :, rows], f_s.at[e, cc, hf], f_r.at[e, cc, hf], beside
        )

    def add_x(i, halves):
        zq = ranked(i)
        e = zq % 2
        first, count = halves[0] * HALF, len(halves) * HALF
        rows = slice(first, first + count)
        for cc in (c, oc):
            for side in (0, 1) if cc is c else (0, 1, 2):
                for hf in halves:
                    ref = rx.at[side, cc, zq, :, rows_of(hf)]
                    pltpu.make_async_copy(ref, ref, x_r.at[side, cc, zq, hf]).wait()
            if cc is c:
                total = psend[x // 2, 4 * (x % 2) + zq, pl.ds(2 * c, 2), rows].astype(F32)
            else:
                total = rx[2, cc, zq, :, rows].astype(F32)
            for side in (0, 1):
                total = total + rx[side, cc, zq, :, rows].astype(F32)

            @pl.when(zq // 2 == yl)
            def _():
                keep[e, cc, :, rows] = total

            @pl.when(zq // 2 != yl)
            def _():
                ysend[e, cc, :, rows] = total.astype(BF16)
                for hf in halves:
                    y_copy(e, cc, hf).start()

    def add_y(i):
        zq = ranked(i)
        e = zq % 2

        @pl.when(zq // 2 == yl)
        def _():
            for hf in (0, 1):
                for cc in (0, 1):
                    y_copy(e, cc, hf).wait_recv()
                    rows = pl.ds(pl.multiple_of(e * 2 * QD + cc * QD + hf * HALF, HALF), HALF)
                    part = slice(hf * HALF, (hf + 1) * HALF)
                    for half in (0, 1):
                        out_buf[rows, half * 256 : (half + 1) * 256] = (
                            keep[e, cc, half, part] + ry[e, cc, half, part].astype(F32)
                        ).astype(BF16)

    def proj_group(k, carry):
        for i in range(7):

            @pl.when(k == i)
            def _():
                before(ga, i)


        project(group_z(k), (0, 1))
        for i in range(1, 7):

            @pl.when(k == i)
            def _():
                relay_x(group_z(i - 1), (0, 1))

        return carry

    lax.fori_loop(0, 7, proj_group, 0)
    def x_done(k, carry):
        zo = group_z(k)

        @pl.when(zo // 4 == x % 2)
        def _():
            for hf in (0, 1):
                to_relay(zo, hf).wait_send()
                to_self(zo, hf).wait_send()

        @pl.when(zo // 4 != x % 2)
        def _():
            for hf in (0, 1):
                for up in (False, True):
                    for other in (0, 1):
                        to_owner(zo, hf, up, other).wait_send()

        return carry

    last = group_z(7)
    ga.forward((0, 1), 4)
    project(last, (0,))
    add_x(0, (0, 1))
    relay_x(group_z(6), (0, 1))
    gk.finish()
    ga.forward((3,), 4)
    project(last, (1,))
    relay_x(last, (0,))
    add_x(1, (0, 1))
    relay_x(last, (1,))
    ga.finish()
    lax.fori_loop(0, 6, x_done, 0)
    add_x(2, (0, 1))
    for hf in (0, 1):
        add_x(3, (hf,))
    for i in range(4):
        add_y(i)
    proj_out = pltpu.make_async_copy(out_buf, out_hbm, out_sem.at[1])
    proj_out.start()

    for e in (0, 1):
        for cc in (0, 1):
            for hf in (0, 1):
                y_copy(e, cc, hf).wait_send()

    lax.fori_loop(6, 8, x_done, 0)
    att_out.wait()
    proj_out.wait()


def per_device(queries, new_keys, new_values, segment_ids, cache_keys, cache_values, cache_lengths, o_weight):
    any_ = pl.BlockSpec(memory_space=pl.ANY)
    vmem = pl.BlockSpec(memory_space=pltpu.VMEM)
    smem = pl.BlockSpec(memory_space=pltpu.SMEM)
    dma = pltpu.SemaphoreType.DMA
    att, out = pl.pallas_call(
        kernel,
        out_shape=(
            jax.ShapeDtypeStruct((ROWS, HD), BF16),
            jax.ShapeDtypeStruct((4 * QD, 512), BF16),
        ),
        in_specs=[any_, any_, any_, vmem, any_, any_, smem, any_],
        out_specs=(any_, any_),
        scratch_shapes=[
            pltpu.VMEM((2, 2, NZ, PKT, HD), BF16),
            pltpu.VMEM((ROWS, HD), BF16),
            pltpu.VMEM((ROWS, HD), F32),
            pltpu.VMEM((ROWS, HD), F32),
            pltpu.VMEM((ROWS, 2 * HD), F32),
            pltpu.VMEM((2, RCHUNK, 5 * CD), F32),
            pltpu.VMEM((2, RCHUNK, HD), F32),
            pltpu.VMEM((5 * CD, 2 * HD), BF16),
            pltpu.VMEM((4, HEADS * HD, 256), BF16),
            pltpu.VMEM((2, NZ, PAIRS, QD, 256), BF16),
            pltpu.VMEM((ROWS, HD), F32),
            pltpu.VMEM((ROWS, HD), BF16),
            pltpu.VMEM((2, NZ, 4, QD, 256), BF16),
            pltpu.VMEM((4, 2, 4, HALF, 256), BF16),
            pltpu.VMEM((3, 2, 4, 2, QD, 256), BF16),
            pltpu.VMEM((2, 2, 2, QD, 256), F32),
            pltpu.VMEM((2, 2, 2, QD, 256), BF16),
            pltpu.VMEM((2, 2, 2, QD, 256), BF16),
            pltpu.VMEM((4 * QD, 512), BF16),
            dma((5,)), dma((2,)), dma((2,)),
            dma((2, 4, 3)), dma((2, 4, 3)), dma((10,)), dma((10,)), dma((4, 9)), dma((4, 9)),
            dma((2, 4, 4)), dma((2, 4, 4)), dma((10,)), dma((10,)),
            dma((NZ, 2, 4)), dma((3, 2, 4, 2)), dma((4, 2)), dma((2, 2, 2)), dma((2, 2, 2)), dma((2,)), dma((2,)),
        ],
        compiler_params=pltpu.CompilerParams(
            collective_id=0, has_side_effects=True, vmem_limit_bytes=56 << 20
        ),
    )(
        queries.reshape(ROWS, HD),
        new_keys.reshape(QD, HD),
        new_values.reshape(QD, HD),
        segment_ids.reshape(1, QD),
        cache_keys.reshape(CD, HD),
        cache_values.reshape(CD, HD),
        cache_lengths,
        o_weight,
    )
    return att.reshape(QD, HEADS, HD), out


def solution(mesh):
    return jax.shard_map(
        per_device,
        mesh=mesh,
        in_specs=(
            P("blk", "head", None),
            P("blk", "head", None),
            P("blk", "head", None),
            P("blk"),
            P("blk", "head", None),
            P("blk", "head", None),
            P("blk"),
            P("head", "blk"),
        ),
        out_specs=(P("blk", "head", None), P("head", "blk")),
        check_vma=False,
    )
```
